256 devices in a mesh: wide: 16 (over z, x_hi), narrow: 16 (over y, x_lo, core).
Axes of the slice: x: 4 (x_hi: 2, x_lo: 2; x = x_hi * 2 + x_lo), y: 4, z: 8, core: 2. Of those that a mesh axis runs over, the one named last changes fastest.
Arguments:
- states: bfloat16 [256, 2097152], P('narrow', 'wide'), may hold values from -6 to 6
- obs_ens: bfloat16 [256, 65536], P('narrow', 'wide'), may hold values from -6 to 6
- obs_value: float32 [65536], P('wide'), may hold values from -6 to 6
- obs_prec: float32 [65536], P('wide'), may hold values from 0.1 to 1
- obs_pick: int32 [256, 1024], P('wide'), may hold values from 0 to 4607, as said below
- taper: float32 [256, 1024], P(('wide', 'narrow')), may hold values from 0.1 to 1
Outputs:
- analysis: bfloat16 [256, 2097152], P('narrow', 'wide')
The draws below stay inside these ranges and needn't reach their ends.
Inputs may be any that keep to these rules, and one draw needn't show every extreme that they name: `obs_pick`: within a region the 1024 rows are distinct.
All inputs are finite; a program needn't handle non-finite values.
Results may differ from the reference program's by a relative error of at most 0.0057.
Values may be sent and summed in bfloat16 or wider, within the bound.
A program may use at most 64 MiB of HBM per device.

```python
import math
import jax
import jax.numpy as jnp
from jax import lax

MEMBERS = 256
CELLS = 8192
OBS_W = 4096
HALO = 256
NPICK = 1024
ITERS = 6
REGIONS = 256
OBS = 65536
N_WIDE = 16
N_NARROW = 16


def draw_obs_pick(key, part):
    keys = jax.random.split(jax.random.fold_in(key, 17), REGIONS)

    def single(region_key):
        return jax.random.permutation(region_key, OBS_W + 2 * HALO)[:NPICK].astype(jnp.int32)
    return jax.vmap(single)(keys)


def block_levels(rng, shape, cuts, smallest, high):
    factor_of = 1.0
    for axis_at, shards_of in cuts:
        draws = jax.random.uniform(jax.random.fold_in(jax.random.fold_in(rng, 6), axis_at), (shards_of,), jnp.float32, smallest / len(cuts), high / len(cuts))
        factor_of = factor_of * jnp.repeat(jnp.exp(draws), shape[axis_at] // shards_of).reshape((-1,) + (1,) * (len(shape) - 1 - axis_at))
    return factor_of


def bell_draw(stream_key, dims, deviation, limit, pieces=(), kind=jnp.bfloat16):
    entries = deviation * jax.random.normal(stream_key, dims, jnp.float32)
    if pieces:
        entries = entries * block_levels(stream_key, dims, pieces, -0.22, 0.18)
    return jnp.clip(entries, -limit, limit).astype(kind)


def setup_inputs(seed: int = 0) -> dict:
    arg_keys = jax.random.split(jax.random.key(seed), 7)
    states = bell_draw(arg_keys[0], (MEMBERS, REGIONS * CELLS), 1.0, 6.0, ((0, 16), (1, 16)))
    obs_ens = bell_draw(arg_keys[1], (MEMBERS, OBS), 1.0, 6.0, ((0, 16), (1, 16)))
    obs_value = bell_draw(arg_keys[2], (OBS,), 1.0, 6.0, ((0, 16),), jnp.float32)
    obs_prec = jnp.clip(jnp.exp(math.log(1.0) - 2.3025851 * jax.random.uniform(arg_keys[3], (OBS,), jnp.float32) ** block_levels(arg_keys[3], (OBS,), ((0, 16),), -0.2, 0.2)), 0.1, 1.0)
    obs_pick = draw_obs_pick(jax.random.fold_in(arg_keys[6], 71), 0)
    taper = jnp.clip(0.1 + 0.9 * jax.random.uniform(arg_keys[5], (REGIONS, NPICK), jnp.float32) ** block_levels(arg_keys[5], (REGIONS, NPICK), ((0, 256),), -0.2, 0.2), 0.1, 1.0)
    return {"states": states, "obs_ens": obs_ens, "obs_value": obs_value, "obs_prec": obs_prec, "obs_pick": obs_pick, "taper": taper}


def analyse(ensemble, observed, precision, taper_row, regional):
    members = ensemble.shape[0]
    obs_mean = lax.optimization_barrier(jnp.mean(ensemble, axis=0))
    obs_pert = ensemble - obs_mean
    obs_weight = precision * taper_row
    scaled = (obs_pert * jnp.sqrt(obs_weight)).astype(jnp.bfloat16)
    identity = jnp.eye(members, dtype=jnp.float32)
    gram_sum = lax.dot_general(scaled, scaled, (((1,), (1,)), ((), ())), preferred_element_type=jnp.float32)
    precision_matrix = gram_sum + (members - 1.0) * identity
    forcing = jnp.dot(obs_pert, obs_weight * (observed - obs_mean), precision=lax.Precision.HIGHEST, preferred_element_type=jnp.float32)
    norm_scale = jnp.sqrt(jnp.sum(precision_matrix * precision_matrix))
    current = precision_matrix / norm_scale
    root_iter = identity
    for iteration in range(ITERS):
        middle = 1.5 * identity - 0.5 * jnp.dot(root_iter, current, precision=lax.Precision.HIGHEST, preferred_element_type=jnp.float32)
        current = jnp.dot(current, middle, precision=lax.Precision.HIGHEST, preferred_element_type=jnp.float32)
        root_iter = jnp.dot(middle, root_iter, precision=lax.Precision.HIGHEST, preferred_element_type=jnp.float32)
    inv_root = root_iter / jnp.sqrt(norm_scale)
    inner = jnp.dot(inv_root, forcing, precision=lax.Precision.HIGHEST, preferred_element_type=jnp.float32)
    mean_weights = jnp.dot(inv_root, inner, precision=lax.Precision.HIGHEST, preferred_element_type=jnp.float32)
    transform = (jnp.sqrt(members - 1.0) * inv_root + mean_weights[:, None]).astype(jnp.bfloat16)
    state_mean = lax.optimization_barrier(jnp.mean(regional.astype(jnp.float32), axis=0))
    state_pert = (regional.astype(jnp.float32) - state_mean).astype(jnp.bfloat16)
    mixed = lax.dot_general(transform, state_pert, (((0,), (0,)), ((), ())), preferred_element_type=jnp.float32)
    return (state_mean + mixed).astype(jnp.bfloat16)

def reference(states, obs_ens, obs_value, obs_prec, obs_pick, taper):
    total_obs = OBS_W * N_WIDE

    def region(index):
        band = index // N_NARROW
        columns = ((band * OBS_W - HALO + obs_pick[index]) % total_obs).astype(jnp.int32)
        ensemble = jnp.take(obs_ens, columns, axis=1).astype(jnp.float32)
        observed = jnp.take(obs_value, columns)
        precision = jnp.take(obs_prec, columns)
        regional = lax.dynamic_slice_in_dim(states, (index * CELLS).astype(jnp.int32), CELLS, 1)
        return analyse(ensemble, observed, precision, taper[index], regional)
    result = lax.map(region, jnp.arange(REGIONS, dtype=jnp.int32))
    members = states.shape[0]
    return jnp.transpose(result, (1, 0, 2)).reshape(members, REGIONS * CELLS)
```

```python
import functools
import math

import jax
import jax.numpy as jnp
from jax import lax
from jax.experimental import pallas as pl
from jax.experimental.pallas import tpu as pltpu
from jax.sharding import PartitionSpec as P

MEMBERS = 256
OWN = 16
CELLS = 8192
OBS_W = 4096
HALO = 256
WIN = OBS_W + 2 * HALO
NPICK = 1024
ITERS = 6
N_WIDE = 16
N_NARROW = 16
LANES = 128
WIN_ROWS = WIN // LANES
CHUNKS = 8
CHUNK = CELLS // CHUNKS
TILE = 256
MESH = pl.DeviceIdType.MESH
HIGH = lax.Precision.HIGHEST
NT = (((1,), (1,)), ((), ()))

PEERS = [
    (dy, dx, dc)
    for dy in (2, 1, 3, 0)
    for dx in (1, 0)
    for dc in (1, 0)
    if (dy, dx, dc) != (0, 0, 0)
]


def kernel(states, obs, value, prec, pick, taper, out,
           inbuf, outbuf, win, vtiles, ptiles, vwin, pwin, tapwin, gram, facc, trans,
           in_send, in_recv, out_send, out_recv, loc_sem, halo_send, halo_recv, obs_send, obs_recv):
    w = lax.axis_index("wide")
    n = lax.axis_index("narrow")
    y, x, c = n // 4, (n // 2) % 2, n % 2

    def at(dy, dx, dc):
        yy, xx, cc = (y + dy) % 4, (x + dx) % 2, (c + dc) % 2
        return 4 * yy + 2 * xx + cc, 4 * yy + 2 * cc + xx

    peers = [at(*d) for d in PEERS]
    before, after = (w + N_WIDE - 1) % N_WIDE, (w + 1) % N_WIDE
    me = 4 * y + 2 * c + x

    def rows(slot, count=1):
        return pl.ds(pl.multiple_of(slot * OWN, OWN), count * OWN)

    barrier = pltpu.get_barrier_semaphore()
    for index, _ in peers:
        pl.semaphore_signal(barrier, inc=1, device_id=(w, index), device_id_type=MESH)
    for band in (before, after):
        pl.semaphore_signal(barrier, inc=1, device_id=(band, n), device_id_type=MESH)
    pl.semaphore_wait(barrier, len(PEERS) + 2)

    def remote(src, dst, send, recv, device):
        return pltpu.make_async_remote_copy(
            src_ref=src, dst_ref=dst, send_sem=send, recv_sem=recv, device_id=device, device_id_type=MESH
        )

    mine = rows(me)
    halos = [
        remote(obs.at[:, pl.ds(OBS_W - HALO, HALO)], win.at[mine, pl.ds(0, HALO)],
               halo_send.at[0], halo_recv.at[0], (after, n)),
        remote(obs.at[:, pl.ds(0, HALO)], win.at[mine, pl.ds(HALO + OBS_W, HALO)],
               halo_send.at[1], halo_recv.at[1], (before, n)),
        remote(value.at[pl.ds(24, 8)], vtiles.at[0], halo_send.at[2], halo_recv.at[2], (after, n)),
        remote(value.at[pl.ds(0, 8)], vtiles.at[1], halo_send.at[3], halo_recv.at[3], (before, n)),
        remote(prec.at[pl.ds(24, 8)], ptiles.at[0], halo_send.at[4], halo_recv.at[4], (after, n)),
        remote(prec.at[pl.ds(0, 8)], ptiles.at[1], halo_send.at[5], halo_recv.at[5], (before, n)),
    ]
    for copy in halos:
        copy.start()
    own_obs = pltpu.make_async_copy(obs, win.at[mine, pl.ds(HALO, OBS_W)], loc_sem.at[0])
    own_obs.start()
    own_states = pltpu.make_async_copy(
        states.at[:, pl.ds(pl.multiple_of(n * CELLS, CELLS), CELLS)], inbuf.at[mine], loc_sem.at[1]
    )
    own_states.start()

    def send_states(chunk):
        for index, _ in peers:
            start = pl.multiple_of(index * CELLS + chunk * CHUNK, CHUNK)
            remote(states.at[:, pl.ds(start, CHUNK)],
                   inbuf.at[mine, pl.ds(pl.multiple_of(chunk * CHUNK, CHUNK), CHUNK)],
                   in_send.at[chunk], in_recv.at[chunk], (w, index)).start()

    send_states(0)

    def move(slot, count, index, sem):
        block = win.at[rows(slot, count)]
        return remote(block, block, obs_send.at[sem], obs_recv.at[sem], (w, index))

    other_core, _ = at(0, 0, 1)
    x_peer, _ = at(0, 1, 0)
    up, _ = at(1, 0, 0)
    down, _ = at(3, 0, 0)

    def pair(dy):
        return 4 * ((y + dy) % 4) + 2 * c

    own_obs.wait()
    halos[0].wait_recv()
    halos[1].wait_recv()
    to_x = move(me, 1, x_peer, 0)
    to_x.start()
    send_states(1)
    to_x.wait_recv()
    to_up = move(pair(0), 2, up, 1)
    to_down = move(pair(0), 2, down, 2)
    to_core0 = move(pair(0), 2, other_core, 3)
    to_up.start()
    to_down.start()
    to_core0.start()
    send_states(2)
    to_up.wait_recv()
    on_up = move(pair(3), 1, up, 4)
    on_up.start()
    to_core1 = move(pair(3), 2, other_core, 5)
    to_core1.start()
    to_down.wait_recv()
    on_down = move(pair(1) + 1, 1, down, 6)
    on_down.start()
    to_core2 = move(pair(1), 2, other_core, 7)
    to_core2.start()
    send_states(3)
    on_up.wait_recv()
    on_down.wait_recv()
    to_core3 = move(pair(2), 2, other_core, 8)
    to_core3.start()

    @pl.loop(4, CHUNKS)
    def _(chunk):
        send_states(chunk)

    for copy in halos[2:]:
        copy.wait_recv()
    vwin[0:2] = vtiles[0, 6:8]
    vwin[2:34] = value[...]
    vwin[34:36] = vtiles[1, 0:2]
    pwin[0:2] = ptiles[0, 6:8]
    pwin[2:34] = prec[...]
    pwin[34:36] = ptiles[1, 0:2]
    own_pick = pick[pl.ds(n, 1), :]
    coarse = lax.broadcasted_iota(jnp.int32, (40, NPICK), 0) == (own_pick >> 7)
    fine = lax.broadcasted_iota(jnp.int32, (LANES, NPICK), 0) == (own_pick & 127)
    tapwin[...] = lax.dot_general(
        jnp.where(coarse, taper[...], 0.0), fine.astype(jnp.float32), NT,
        precision=HIGH, preferred_element_type=jnp.float32,
    )
    gram[...] = jnp.zeros_like(gram)
    facc[...] = jnp.zeros_like(facc)
    for copy in (to_core0, to_core1, to_core2, to_core3):
        copy.wait_recv()

    @pl.loop(0, WIN // TILE)
    def _(tile):
        columns = pl.ds(pl.multiple_of(tile * TILE, TILE), TILE)

        def flat(ref):
            return jnp.concatenate([ref[pl.ds(2 * tile, 1), :], ref[pl.ds(2 * tile + 1, 1), :]], axis=1)

        ensemble = win[:, columns].astype(jnp.float32)
        mean = jnp.sum(ensemble, axis=0, keepdims=True) * (1.0 / MEMBERS)
        pert = ensemble - mean
        weight = flat(pwin) * flat(tapwin)
        scaled = (pert * jnp.sqrt(weight)).astype(jnp.bfloat16)
        gram[...] += lax.dot_general(scaled, scaled, NT, preferred_element_type=jnp.float32)
        force = pert * (weight * (flat(vwin) - mean))
        facc[...] += force[:, :LANES] + force[:, LANES:]

    identity = (
        lax.broadcasted_iota(jnp.int32, (MEMBERS, MEMBERS), 0)
        == lax.broadcasted_iota(jnp.int32, (MEMBERS, MEMBERS), 1)
    ).astype(jnp.float32)

    def dot(a, b):
        return jnp.dot(a, b, precision=HIGH, preferred_element_type=jnp.float32)

    matrix = gram[...] + (MEMBERS - 1.0) * identity
    scale = jnp.sqrt(jnp.sum(jnp.sum(matrix * matrix, axis=0, keepdims=True), axis=1, keepdims=True))
    gram[...] = matrix / scale
    trans[...] = identity

    @pl.loop(0, ITERS)
    def _(_):
        current, root = gram[...], trans[...]
        middle = 1.5 * identity - 0.5 * dot(root, current)
        gram[...] = dot(current, middle)
        trans[...] = dot(middle, root)

    inv_root = trans[...] / jnp.sqrt(scale)
    force = lax.dot_general(
        jnp.ones((8, LANES), jnp.float32), facc[...], NT, precision=HIGH, preferred_element_type=jnp.float32
    )
    inner = lax.dot_general(force, inv_root, NT, precision=HIGH, preferred_element_type=jnp.float32)
    weights = lax.dot_general(inner, inv_root, NT, precision=HIGH, preferred_element_type=jnp.float32)
    transform = (math.sqrt(MEMBERS - 1.0) * inv_root + weights[0:1]).astype(jnp.bfloat16)
    trans[...] = transform.astype(jnp.float32)
    own_states.wait()

    @pl.loop(0, CHUNKS)
    def _(chunk):
        columns = pl.ds(pl.multiple_of(chunk * CHUNK, CHUNK), CHUNK)
        arrived = inbuf.at[pl.ds(0, MEMBERS - OWN), columns]
        pltpu.make_async_copy(arrived, arrived, in_recv.at[chunk]).wait()
        mixer = trans[...].astype(jnp.bfloat16)

        @pl.loop(0, CHUNK // TILE)
        def _(tile):
            part = pl.ds(pl.multiple_of(chunk * CHUNK + tile * TILE, TILE), TILE)
            entries = inbuf[:, part].astype(jnp.float32)
            mean = jnp.sum(entries, axis=0, keepdims=True) * (1.0 / MEMBERS)
            pert = (entries - mean).astype(jnp.bfloat16)
            mixed = jnp.dot(mixer, pert, preferred_element_type=jnp.float32)
            outbuf[:, part] = (mean + mixed).astype(jnp.bfloat16)

        target = pl.ds(pl.multiple_of(n * CELLS + chunk * CHUNK, CHUNK), CHUNK)
        for index, slot in peers:
            remote(outbuf.at[rows(slot), columns], out.at[:, target],
                   out_send.at[chunk], out_recv.at[chunk], (w, index)).start()

    own_out = pltpu.make_async_copy(
        outbuf.at[mine], out.at[:, pl.ds(pl.multiple_of(n * CELLS, CELLS), CELLS)], loc_sem.at[2]
    )
    own_out.start()
    for copy in halos:
        copy.wait_send()
    for copy in (to_x, to_up, to_down, on_up, on_down, to_core0, to_core1, to_core2, to_core3):
        copy.wait_send()

    @pl.loop(0, CHUNKS)
    def _(chunk):
        columns = pl.ds(pl.multiple_of(chunk * CHUNK, CHUNK), CHUNK)
        most = outbuf.at[pl.ds(0, MEMBERS - OWN), columns]
        pltpu.make_async_copy(most, most, in_send.at[chunk]).wait()
        pltpu.make_async_copy(most, most, out_send.at[chunk]).wait()
        pltpu.make_async_copy(most, most, out_recv.at[chunk]).wait()

    own_out.wait()


def body(states, obs_ens, obs_value, obs_prec, obs_pick, taper):
    vmem, hbm = (pl.BlockSpec(memory_space=pltpu.VMEM), pl.BlockSpec(memory_space=pl.ANY))
    dma = pltpu.SemaphoreType.DMA
    return pl.pallas_call(
        kernel,
        out_shape=jax.ShapeDtypeStruct(states.shape, jnp.bfloat16),
        in_specs=[hbm, vmem, vmem, vmem, vmem, vmem],
        out_specs=hbm,
        scratch_shapes=[
            pltpu.VMEM((MEMBERS, CELLS), jnp.bfloat16),
            pltpu.VMEM((MEMBERS, CELLS), jnp.bfloat16),
            pltpu.VMEM((MEMBERS, WIN), jnp.bfloat16),
            pltpu.VMEM((2, 8, LANES), jnp.float32),
            pltpu.VMEM((2, 8, LANES), jnp.float32),
            pltpu.VMEM((40, LANES), jnp.float32),
            pltpu.VMEM((40, LANES), jnp.float32),
            pltpu.VMEM((40, LANES), jnp.float32),
            pltpu.VMEM((MEMBERS, MEMBERS), jnp.float32),
            pltpu.VMEM((MEMBERS, LANES), jnp.float32),
            pltpu.VMEM((MEMBERS, MEMBERS), jnp.float32),
            dma((CHUNKS,)),
            dma((CHUNKS,)),
            dma((CHUNKS,)),
            dma((CHUNKS,)),
            dma((3,)),
            dma((6,)),
            dma((6,)),
            dma((9,)),
            dma((9,)),
        ],
        compiler_params=pltpu.CompilerParams(
            collective_id=0, has_side_effects=True, vmem_limit_bytes=40 << 20
        ),
        name="analysis",
    )(states, obs_ens, obs_value.reshape(OBS_W // LANES, LANES), obs_prec.reshape(OBS_W // LANES, LANES), obs_pick, taper)


def solution(mesh):
    return jax.shard_map(
        body,
        mesh=mesh,
        in_specs=(
            P("narrow", "wide"),
            P("narrow", "wide"),
            P("wide"),
            P("wide"),
            P("wide", None),
            P(("wide", "narrow"), None),
        ),
        out_specs=P("narrow", "wide"),
        check_vma=False,
    )
```

```python
import functools
import math

import jax
import jax.numpy as jnp
from jax import lax
from jax.experimental import pallas as pl
from jax.experimental.pallas import tpu as pltpu
from jax.sharding import PartitionSpec as P

MEMBERS = 256
OWN = 16
CELLS = 8192
OBS_W = 4096
HALO = 256
WIN = OBS_W + 2 * HALO
NPICK = 1024
ITERS = 6
N_WIDE = 16
N_NARROW = 16
LANES = 128
WIN_ROWS = WIN // LANES
CHUNKS = 8
CHUNK = CELLS // CHUNKS
TILE = 256
MESH = pl.DeviceIdType.MESH
HIGH = lax.Precision.HIGHEST
NT = (((1,), (1,)), ((), ()))

PEERS = [
    (dy, dx, dc)
    for dy in (2, 1, 3, 0)
    for dx in (1, 0)
    for dc in (1, 0)
    if (dy, dx, dc) != (0, 0, 0)
]


def kernel(states, obs, value, prec, pick, taper, out,
           inbuf, outbuf, win, vwin, pwin, picked, tap, tapwin, gram, facc, trans,
           in_send, in_recv, out_send, out_recv, loc_sem, halo_send, halo_recv, obs_send, obs_recv):
    w = lax.axis_index("wide")
    n = lax.axis_index("narrow")
    y, x, c = n // 4, (n // 2) % 2, n % 2

    def at(dy, dx, dc):
        yy, xx, cc = (y + dy) % 4, (x + dx) % 2, (c + dc) % 2
        return 4 * yy + 2 * xx + cc, 4 * yy + 2 * cc + xx

    peers = [at(*d) for d in PEERS]
    before, after = (w + N_WIDE - 1) % N_WIDE, (w + 1) % N_WIDE
    me = 4 * y + 2 * c + x

    def rows(slot, count=1):
        return pl.ds(pl.multiple_of(slot * OWN, OWN), count * OWN)

    barrier = pltpu.get_barrier_semaphore()
    for index, _ in peers:
        pl.semaphore_signal(barrier, inc=1, device_id=(w, index), device_id_type=MESH)
    pl.semaphore_signal(barrier, inc=1, device_id=(before, n), device_id_type=MESH)
    pl.semaphore_wait(barrier, len(PEERS) + 1)

    def remote(src, dst, send, recv, device):
        return pltpu.make_async_remote_copy(
            src_ref=src, dst_ref=dst, send_sem=send, recv_sem=recv, device_id=device, device_id_type=MESH
        )

    mine = rows(me)
    halos = [
        remote(obs.at[:, pl.ds(OBS_W - HALO, HALO)], win.at[mine, pl.ds(0, HALO)],
               halo_send.at[0], halo_recv.at[0], (after, n)),
        remote(obs.at[:, pl.ds(0, HALO)], win.at[mine, pl.ds(HALO + OBS_W, HALO)],
               halo_send.at[1], halo_recv.at[1], (before, n)),
        remote(value.at[pl.ds(24, 8)], vwin.at[pl.ds(0, 8)], halo_send.at[2], halo_recv.at[2], (after, n)),
        remote(value.at[pl.ds(0, 8)], vwin.at[pl.ds(40, 8)], halo_send.at[3], halo_recv.at[3], (before, n)),
        remote(prec.at[pl.ds(24, 8)], pwin.at[pl.ds(0, 8)], halo_send.at[4], halo_recv.at[4], (after, n)),
        remote(prec.at[pl.ds(0, 8)], pwin.at[pl.ds(40, 8)], halo_send.at[5], halo_recv.at[5], (before, n)),
    ]
    for copy in halos[0::2]:
        copy.start()
    own_obs = pltpu.make_async_copy(obs, win.at[mine, pl.ds(HALO, OBS_W)], loc_sem.at[0])
    own_obs.start()
    own_states = pltpu.make_async_copy(
        states.at[:, pl.ds(pl.multiple_of(n * CELLS, CELLS), CELLS)], inbuf.at[mine], loc_sem.at[1]
    )
    own_states.start()
    smalls = [
        pltpu.make_async_copy(value, vwin.at[pl.ds(8, 32)], loc_sem.at[3]),
        pltpu.make_async_copy(prec, pwin.at[pl.ds(8, 32)], loc_sem.at[4]),
        pltpu.make_async_copy(pick.at[pl.ds(pl.multiple_of(n // 8 * 8, 8), 8)], picked, loc_sem.at[5]),
        pltpu.make_async_copy(taper, tap, loc_sem.at[6]),
    ]
    for copy in smalls:
        copy.start()

    def send_states(chunk):
        for index, _ in peers:
            start = pl.multiple_of(index * CELLS + chunk * CHUNK, CHUNK)
            remote(states.at[:, pl.ds(start, CHUNK)],
                   inbuf.at[mine, pl.ds(pl.multiple_of(chunk * CHUNK, CHUNK), CHUNK)],
                   in_send.at[chunk], in_recv.at[chunk], (w, index)).start()

    send_states(0)

    def move(slot, count, index, sem):
        block = win.at[rows(slot, count)]
        return remote(block, block, obs_send.at[sem], obs_recv.at[sem], (w, index))

    other_core, _ = at(0, 0, 1)
    x_peer, _ = at(0, 1, 0)
    up, _ = at(1, 0, 0)
    down, _ = at(3, 0, 0)

    def pair(dy):
        return 4 * ((y + dy) % 4) + 2 * c

    own_obs.wait()
    halos[0].wait_recv()
    for copy in halos[1::2]:
        copy.start()
    halos[1].wait_recv()
    to_x = move(me, 1, x_peer, 0)
    to_x.start()
    send_states(1)
    to_x.wait_recv()
    to_up = move(pair(0), 2, up, 1)
    to_down = move(pair(0), 2, down, 2)
    to_core0 = move(pair(0), 2, other_core, 3)
    to_up.start()
    to_down.start()
    to_core0.start()
    send_states(2)
    to_up.wait_recv()
    on_up = move(pair(3), 1, up, 4)
    on_up.start()
    to_core1 = move(pair(3), 2, other_core, 5)
    to_core1.start()
    to_down.wait_recv()
    on_down = move(pair(1) + 1, 1, down, 6)
    on_down.start()
    to_core2 = move(pair(1), 2, other_core, 7)
    to_core2.start()
    send_states(3)
    on_up.wait_recv()
    on_down.wait_recv()
    to_core3 = move(pair(2), 2, other_core, 8)
    to_core3.start()

    @pl.loop(4, CHUNKS)
    def _(chunk):
        send_states(chunk)

    for copy in smalls:
        copy.wait()
    own_pick = picked[pl.ds(n % 8, 1), :]
    coarse = lax.broadcasted_iota(jnp.int32, (40, NPICK), 0) == (own_pick >> 7)
    fine = lax.broadcasted_iota(jnp.int32, (LANES, NPICK), 0) == (own_pick & 127)
    tapwin[...] = lax.dot_general(
        jnp.where(coarse, tap[...], 0.0), fine.astype(jnp.float32), NT,
        precision=HIGH, preferred_element_type=jnp.float32,
    )
    gram[...] = jnp.zeros_like(gram)
    facc[...] = jnp.zeros_like(facc)
    for copy in halos[2:]:
        copy.wait_recv()
    for copy in (to_core0, to_core1, to_core2, to_core3):
        copy.wait_recv()

    @pl.loop(0, WIN // TILE)
    def _(tile):
        columns = pl.ds(pl.multiple_of(tile * TILE, TILE), TILE)

        def flat(ref, first):
            row = first + 2 * tile
            return jnp.concatenate([ref[pl.ds(row, 1), :], ref[pl.ds(row + 1, 1), :]], axis=1)

        ensemble = win[:, columns].astype(jnp.float32)
        mean = jnp.sum(ensemble, axis=0, keepdims=True) * (1.0 / MEMBERS)
        pert = ensemble - mean
        weight = flat(pwin, 6) * flat(tapwin, 0)
        scaled = (pert * jnp.sqrt(weight)).astype(jnp.bfloat16)
        gram[...] += lax.dot_general(scaled, scaled, NT, preferred_element_type=jnp.float32)
        force = pert * (weight * (flat(vwin, 6) - mean))
        facc[...] += force[:, :LANES] + force[:, LANES:]

    identity = (
        lax.broadcasted_iota(jnp.int32, (MEMBERS, MEMBERS), 0)
        == lax.broadcasted_iota(jnp.int32, (MEMBERS, MEMBERS), 1)
    ).astype(jnp.float32)

    def dot(a, b):
        return jnp.dot(a, b, precision=HIGH, preferred_element_type=jnp.float32)

    matrix = gram[...] + (MEMBERS - 1.0) * identity
    scale = jnp.sqrt(jnp.sum(jnp.sum(matrix * matrix, axis=0, keepdims=True), axis=1, keepdims=True))
    gram[...] = matrix / scale
    trans[...] = identity

    @pl.loop(0, ITERS)
    def _(_):
        current, root = gram[...], trans[...]
        middle = 1.5 * identity - 0.5 * dot(root, current)
        gram[...] = dot(current, middle)
        trans[...] = dot(middle, root)

    inv_root = trans[...] / jnp.sqrt(scale)
    force = lax.dot_general(
        jnp.ones((8, LANES), jnp.float32), facc[...], NT, precision=HIGH, preferred_element_type=jnp.float32
    )
    inner = lax.dot_general(force, inv_root, NT, precision=HIGH, preferred_element_type=jnp.float32)
    weights = lax.dot_general(inner, inv_root, NT, precision=HIGH, preferred_element_type=jnp.float32)
    transform = (math.sqrt(MEMBERS - 1.0) * inv_root + weights[0:1]).astype(jnp.bfloat16)
    trans[...] = transform.astype(jnp.float32)
    own_states.wait()

    @pl.loop(0, CHUNKS)
    def _(chunk):
        columns = pl.ds(pl.multiple_of(chunk * CHUNK, CHUNK), CHUNK)
        arrived = inbuf.at[pl.ds(0, MEMBERS - OWN), columns]
        pltpu.make_async_copy(arrived, arrived, in_recv.at[chunk]).wait()
        mixer = trans[...].astype(jnp.bfloat16)

        @pl.loop(0, CHUNK // TILE)
        def _(tile):
            part = pl.ds(pl.multiple_of(chunk * CHUNK + tile * TILE, TILE), TILE)
            entries = inbuf[:, part].astype(jnp.float32)
            mean = jnp.sum(entries, axis=0, keepdims=True) * (1.0 / MEMBERS)
            pert = (entries - mean).astype(jnp.bfloat16)
            mixed = jnp.dot(mixer, pert, preferred_element_type=jnp.float32)
            outbuf[:, part] = (mean + mixed).astype(jnp.bfloat16)

        target = pl.ds(pl.multiple_of(n * CELLS + chunk * CHUNK, CHUNK), CHUNK)
        for index, slot in peers:
            remote(outbuf.at[rows(slot), columns], out.at[:, target],
                   out_send.at[chunk], out_recv.at[chunk], (w, index)).start()

    own_out = pltpu.make_async_copy(
        outbuf.at[mine], out.at[:, pl.ds(pl.multiple_of(n * CELLS, CELLS), CELLS)], loc_sem.at[2]
    )
    own_out.start()
    for copy in halos:
        copy.wait_send()
    for copy in (to_x, to_up, to_down, on_up, on_down, to_core0, to_core1, to_core2, to_core3):
        copy.wait_send()

    @pl.loop(0, CHUNKS)
    def _(chunk):
        columns = pl.ds(pl.multiple_of(chunk * CHUNK, CHUNK), CHUNK)
        most = outbuf.at[pl.ds(0, MEMBERS - OWN), columns]
        pltpu.make_async_copy(most, most, in_send.at[chunk]).wait()
        pltpu.make_async_copy(most, most, out_send.at[chunk]).wait()
        pltpu.make_async_copy(most, most, out_recv.at[chunk]).wait()

    own_out.wait()


def body(states, obs_ens, obs_value, obs_prec, obs_pick, taper):
    hbm, anywhere = (pl.BlockSpec(memory_space=pltpu.HBM), pl.BlockSpec(memory_space=pl.ANY))
    dma = pltpu.SemaphoreType.DMA
    return pl.pallas_call(
        kernel,
        out_shape=jax.ShapeDtypeStruct(states.shape, jnp.bfloat16),
        in_specs=[hbm] * 6,
        out_specs=anywhere,
        scratch_shapes=[
            pltpu.VMEM((MEMBERS, CELLS), jnp.bfloat16),
            pltpu.VMEM((MEMBERS, CELLS), jnp.bfloat16),
            pltpu.VMEM((MEMBERS, WIN), jnp.bfloat16),
            pltpu.VMEM((48, LANES), jnp.float32),
            pltpu.VMEM((48, LANES), jnp.float32),
            pltpu.VMEM((8, NPICK), jnp.int32),
            pltpu.VMEM((1, NPICK), jnp.float32),
            pltpu.VMEM((40, LANES), jnp.float32),
            pltpu.VMEM((MEMBERS, MEMBERS), jnp.float32),
            pltpu.VMEM((MEMBERS, LANES), jnp.float32),
            pltpu.VMEM((MEMBERS, MEMBERS), jnp.float32),
            dma((CHUNKS,)),
            dma((CHUNKS,)),
            dma((CHUNKS,)),
            dma((CHUNKS,)),
            dma((7,)),
            dma((6,)),
            dma((6,)),
            dma((9,)),
            dma((9,)),
        ],
        compiler_params=pltpu.CompilerParams(
            collective_id=0, has_side_effects=True, vmem_limit_bytes=48 << 20
        ),
        name="analysis",
    )(states, obs_ens, obs_value.reshape(OBS_W // LANES, LANES), obs_prec.reshape(OBS_W // LANES, LANES), obs_pick, taper)


def solution(mesh):
    return jax.shard_map(
        body,
        mesh=mesh,
        in_specs=(
            P("narrow", "wide"),
            P("narrow", "wide"),
            P("wide"),
            P("wide"),
            P("wide", None),
            P(("wide", "narrow"), None),
        ),
        out_specs=P("narrow", "wide"),
        check_vma=False,
    )
```

```python
import functools
import math

import jax
import jax.numpy as jnp
from jax import lax
from jax.experimental import pallas as pl
from jax.experimental.pallas import tpu as pltpu
from jax.sharding import PartitionSpec as P

MEMBERS = 256
OWN = 16
CELLS = 8192
OBS_W = 4096
HALO = 256
WIN = OBS_W + 2 * HALO
NPICK = 1024
ITERS = 6
N_WIDE = 16
N_NARROW = 16
LANES = 128
WIN_ROWS = WIN // LANES
CHUNKS = 8
CHUNK = CELLS // CHUNKS
TILE = 256
MESH = pl.DeviceIdType.MESH
HIGH = lax.Precision.HIGHEST
NT = (((1,), (1,)), ((), ()))

PEERS = [
    (1, 0, 0), (0, 1, 0), (3, 0, 1), (2, 1, 1), (1, 0, 1), (0, 1, 1), (3, 0, 0), (2, 0, 0),
    (1, 1, 0), (2, 0, 1), (3, 1, 1), (1, 1, 1), (2, 1, 0), (3, 1, 0), (0, 0, 1),
]


def kernel(states, obs, small, out,
           inbuf, outbuf, win, vwin, pwin, picks, tapwin, gram, facc, trans,
           in_send, in_recv, out_send, out_recv, loc_sem, halo_send, halo_recv, obs_send, obs_recv):
    w = lax.axis_index("wide")
    n = lax.axis_index("narrow")
    y, x, c = n // 4, (n // 2) % 2, n % 2

    def at(dy, dx, dc):
        yy, xx, cc = (y + dy) % 4, (x + dx) % 2, (c + dc) % 2
        return 4 * yy + 2 * xx + cc, 4 * yy + 2 * cc + xx

    peers = [at(*d) for d in PEERS]
    before, after = (w + N_WIDE - 1) % N_WIDE, (w + 1) % N_WIDE
    me = 4 * y + 2 * c + x

    def rows(slot, count=1):
        return pl.ds(pl.multiple_of(slot * OWN, OWN), count * OWN)

    barrier = pltpu.get_barrier_semaphore()
    for index, _ in peers:
        pl.semaphore_signal(barrier, inc=1, device_id=(w, index), device_id_type=MESH)
    pl.semaphore_signal(barrier, inc=1, device_id=(before, n), device_id_type=MESH)
    pl.semaphore_wait(barrier, len(PEERS) + 1)

    def remote(src, dst, send, recv, device):
        return pltpu.make_async_remote_copy(
            src_ref=src, dst_ref=dst, send_sem=send, recv_sem=recv, device_id=device, device_id_type=MESH
        )

    mine = rows(me)
    halos = [
        remote(obs.at[:, pl.ds(OBS_W - HALO, HALO)], win.at[mine, pl.ds(0, HALO)],
               halo_send.at[0], halo_recv.at[0], (after, n)),
        remote(obs.at[:, pl.ds(0, HALO)], win.at[mine, pl.ds(HALO + OBS_W, HALO)],
               halo_send.at[1], halo_recv.at[1], (before, n)),
        remote(small.at[pl.ds(24, 8)], vwin.at[pl.ds(0, 8)], halo_send.at[2], halo_recv.at[2], (after, n)),
        remote(small.at[pl.ds(0, 8)], vwin.at[pl.ds(40, 8)], halo_send.at[3], halo_recv.at[3], (before, n)),
        remote(small.at[pl.ds(56, 8)], pwin.at[pl.ds(0, 8)], halo_send.at[4], halo_recv.at[4], (after, n)),
        remote(small.at[pl.ds(32, 8)], pwin.at[pl.ds(40, 8)], halo_send.at[5], halo_recv.at[5], (before, n)),
    ]
    for copy in halos[0::2]:
        copy.start()
    own_obs = pltpu.make_async_copy(obs, win.at[mine, pl.ds(HALO, OBS_W)], loc_sem.at[0])
    own_obs.start()
    own_states = pltpu.make_async_copy(
        states.at[:, pl.ds(pl.multiple_of(n * CELLS, CELLS), CELLS)], inbuf.at[mine], loc_sem.at[1]
    )
    own_states.start()
    smalls = [
        pltpu.make_async_copy(small.at[pl.ds(0, 32)], vwin.at[pl.ds(8, 32)], loc_sem.at[3]),
        pltpu.make_async_copy(small.at[pl.ds(32, 32)], pwin.at[pl.ds(8, 32)], loc_sem.at[4]),
        pltpu.make_async_copy(small.at[pl.ds(64, 16)], picks, loc_sem.at[5]),
    ]
    for copy in smalls:
        copy.start()

    def send_states(chunk):
        for index, _ in peers:
            start = pl.multiple_of(index * CELLS + chunk * CHUNK, CHUNK)
            remote(states.at[:, pl.ds(start, CHUNK)],
                   inbuf.at[mine, pl.ds(pl.multiple_of(chunk * CHUNK, CHUNK), CHUNK)],
                   in_send.at[chunk], in_recv.at[chunk], (w, index)).start()

    send_states(0)

    left, right = (0, WIN // 2), (WIN // 2, WIN // 2)
    right_low, right_high = (WIN // 2, WIN // 4), (WIN // 2 + WIN // 4, WIN // 4)

    def move(slot, count, columns, to, sem):
        block = win.at[rows(slot, count), pl.ds(*columns)]
        copy = remote(block, block, obs_send.at[sem], obs_recv.at[sem], (w, at(*to)[0]))
        copy.start()
        moves.append(copy)
        return copy

    def pair(dy):
        return 4 * ((y + dy) % 4) + 2 * c

    def one(dy):
        return pair(dy) + x

    moves = []
    up, down, across, core = (1, 0, 0), (3, 0, 0), (0, 1, 0), (0, 0, 1)
    own_obs.wait()
    halos[0].wait_recv()
    for copy in halos[1::2]:
        copy.start()
    left_x = move(one(0), 1, left, across, 0)
    send_states(1)
    halos[1].wait_recv()
    right_up = move(one(0), 1, right, up, 1)
    right_down = move(one(0), 1, right, down, 2)
    right_x0 = move(one(0), 1, right, across, 3)
    left_x.wait_recv()
    left_up = move(pair(0), 2, left, up, 4)
    left_down = move(pair(0), 2, left, down, 5)
    last = [move(pair(0), 2, left, core, 6)]
    send_states(2)
    right_up.wait_recv()
    right_up2 = move(one(3), 1, right_low, up, 7)
    right_x3 = move(one(3), 1, right, across, 8)
    right_down.wait_recv()
    right_down2 = move(one(1), 1, right_high, down, 9)
    right_x1 = move(one(1), 1, right, across, 10)
    left_up.wait_recv()
    left_up2 = move(pair(3), 1, left, up, 11)
    last.append(move(pair(3), 2, left, core, 12))
    left_down.wait_recv()
    left_down2 = move(pair(1) + 1, 1, left, down, 13)
    last.append(move(pair(1), 2, left, core, 14))
    send_states(3)
    right_up2.wait_recv()
    right_down2.wait_recv()
    right_x2 = move(one(2), 1, right, across, 15)
    right_x0.wait_recv()
    last.append(move(pair(0), 2, right, core, 16))
    right_x3.wait_recv()
    last.append(move(pair(3), 2, right, core, 17))
    right_x1.wait_recv()
    last.append(move(pair(1), 2, right, core, 18))
    left_up2.wait_recv()
    left_down2.wait_recv()
    last.append(move(pair(2), 2, left, core, 19))
    send_states(4)
    right_x2.wait_recv()
    last.append(move(pair(2), 2, right, core, 20))

    @pl.loop(5, CHUNKS)
    def _(chunk):
        send_states(chunk)

    for copy in smalls:
        copy.wait()
    own_taper, own_pick = (
        jnp.concatenate([picks[8 * part + k : 8 * part + k + 1, :] for k in range(8)], axis=1) for part in (0, 1)
    )
    own_pick = own_pick.astype(jnp.int32)
    coarse = lax.broadcasted_iota(jnp.int32, (40, NPICK), 0) == (own_pick >> 7)
    fine = lax.broadcasted_iota(jnp.int32, (LANES, NPICK), 0) == (own_pick & 127)
    tapwin[...] = lax.dot_general(
        jnp.where(coarse, own_taper, 0.0), fine.astype(jnp.float32), NT,
        precision=HIGH, preferred_element_type=jnp.float32,
    )
    gram[...] = jnp.zeros_like(gram)
    facc[...] = jnp.zeros_like(facc)
    for copy in halos[2:]:
        copy.wait_recv()
    for copy in last:
        copy.wait_recv()

    @pl.loop(0, WIN // TILE)
    def _(tile):
        columns = pl.ds(pl.multiple_of(tile * TILE, TILE), TILE)

        def flat(ref, first):
            row = first + 2 * tile
            return jnp.concatenate([ref[pl.ds(row, 1), :], ref[pl.ds(row + 1, 1), :]], axis=1)

        ensemble = win[:, columns].astype(jnp.float32)
        mean = jnp.sum(ensemble, axis=0, keepdims=True) * (1.0 / MEMBERS)
        pert = ensemble - mean
        weight = flat(pwin, 6) * flat(tapwin, 0)
        scaled = (pert * jnp.sqrt(weight)).astype(jnp.bfloat16)
        gram[...] += lax.dot_general(scaled, scaled, NT, preferred_element_type=jnp.float32)
        force = pert * (weight * (flat(vwin, 6) - mean))
        facc[...] += force[:, :LANES] + force[:, LANES:]

    identity = (
        lax.broadcasted_iota(jnp.int32, (MEMBERS, MEMBERS), 0)
        == lax.broadcasted_iota(jnp.int32, (MEMBERS, MEMBERS), 1)
    ).astype(jnp.float32)

    def dot(a, b):
        return jnp.dot(a, b, precision=HIGH, preferred_element_type=jnp.float32)

    matrix = gram[...] + (MEMBERS - 1.0) * identity
    scale = jnp.sqrt(jnp.sum(jnp.sum(matrix * matrix, axis=0, keepdims=True), axis=1, keepdims=True))
    gram[...] = matrix / scale
    trans[...] = identity

    @pl.loop(0, ITERS)
    def _(_):
        current, root = gram[...], trans[...]
        middle = 1.5 * identity - 0.5 * dot(root, current)
        gram[...] = dot(current, middle)
        trans[...] = dot(middle, root)

    inv_root = trans[...] / jnp.sqrt(scale)
    force = lax.dot_general(
        jnp.ones((8, LANES), jnp.float32), facc[...], NT, precision=HIGH, preferred_element_type=jnp.float32
    )
    inner = lax.dot_general(force, inv_root, NT, precision=HIGH, preferred_element_type=jnp.float32)
    weights = lax.dot_general(inner, inv_root, NT, precision=HIGH, preferred_element_type=jnp.float32)
    transform = (math.sqrt(MEMBERS - 1.0) * inv_root + weights[0:1]).astype(jnp.bfloat16)
    trans[...] = transform.astype(jnp.float32)
    own_states.wait()

    @pl.loop(0, CHUNKS)
    def _(chunk):
        columns = pl.ds(pl.multiple_of(chunk * CHUNK, CHUNK), CHUNK)
        arrived = inbuf.at[pl.ds(0, MEMBERS - OWN), columns]
        pltpu.make_async_copy(arrived, arrived, in_recv.at[chunk]).wait()
        mixer = trans[...].astype(jnp.bfloat16)

        @pl.loop(0, CHUNK // TILE)
        def _(tile):
            part = pl.ds(pl.multiple_of(chunk * CHUNK + tile * TILE, TILE), TILE)
            entries = inbuf[:, part].astype(jnp.float32)
            mean = jnp.sum(entries, axis=0, keepdims=True) * (1.0 / MEMBERS)
            pert = (entries - mean).astype(jnp.bfloat16)
            mixed = jnp.dot(mixer, pert, preferred_element_type=jnp.float32)
            outbuf[:, part] = (mean + mixed).astype(jnp.bfloat16)

        target = pl.ds(pl.multiple_of(n * CELLS + chunk * CHUNK, CHUNK), CHUNK)
        for index, slot in peers:
            remote(outbuf.at[rows(slot), columns], out.at[:, target],
                   out_send.at[chunk], out_recv.at[chunk], (w, index)).start()

    own_out = pltpu.make_async_copy(
        outbuf.at[mine], out.at[:, pl.ds(pl.multiple_of(n * CELLS, CELLS), CELLS)], loc_sem.at[2]
    )
    own_out.start()
    for copy in halos:
        copy.wait_send()
    for copy in moves:
        copy.wait_send()

    @pl.loop(0, CHUNKS)
    def _(chunk):
        columns = pl.ds(pl.multiple_of(chunk * CHUNK, CHUNK), CHUNK)
        most = outbuf.at[pl.ds(0, MEMBERS - OWN), columns]
        pltpu.make_async_copy(most, most, in_send.at[chunk]).wait()
        pltpu.make_async_copy(most, most, out_send.at[chunk]).wait()
        pltpu.make_async_copy(most, most, out_recv.at[chunk]).wait()

    own_out.wait()


def body(states, obs_ens, obs_value, obs_prec, obs_pick, taper):
    hbm, anywhere = (pl.BlockSpec(memory_space=pltpu.HBM), pl.BlockSpec(memory_space=pl.ANY))
    dma = pltpu.SemaphoreType.DMA
    own_pick = lax.dynamic_slice_in_dim(obs_pick, lax.axis_index("narrow"), 1, 0)
    small = jnp.concatenate(
        [part.astype(jnp.float32).reshape(-1, LANES) for part in (obs_value, obs_prec, taper, own_pick)], axis=0
    )
    return pl.pallas_call(
        kernel,
        out_shape=jax.ShapeDtypeStruct(states.shape, jnp.bfloat16),
        in_specs=[hbm] * 3,
        out_specs=anywhere,
        scratch_shapes=[
            pltpu.VMEM((MEMBERS, CELLS), jnp.bfloat16),
            pltpu.VMEM((MEMBERS, CELLS), jnp.bfloat16),
            pltpu.VMEM((MEMBERS, WIN), jnp.bfloat16),
            pltpu.VMEM((48, LANES), jnp.float32),
            pltpu.VMEM((48, LANES), jnp.float32),
            pltpu.VMEM((16, LANES), jnp.float32),
            pltpu.VMEM((40, LANES), jnp.float32),
            pltpu.VMEM((MEMBERS, MEMBERS), jnp.float32),
            pltpu.VMEM((MEMBERS, LANES), jnp.float32),
            pltpu.VMEM((MEMBERS, MEMBERS), jnp.float32),
            dma((CHUNKS,)),
            dma((CHUNKS,)),
            dma((CHUNKS,)),
            dma((CHUNKS,)),
            dma((6,)),
            dma((6,)),
            dma((6,)),
            dma((21,)),
            dma((21,)),
        ],
        compiler_params=pltpu.CompilerParams(
            collective_id=0, has_side_effects=True, vmem_limit_bytes=48 << 20
        ),
        name="analysis",
    )(states, obs_ens, small)


def solution(mesh):
    return jax.shard_map(
        body,
        mesh=mesh,
        in_specs=(
            P("narrow", "wide"),
            P("narrow", "wide"),
            P("wide"),
            P("wide"),
            P("wide", None),
            P(("wide", "narrow"), None),
        ),
        out_specs=P("narrow", "wide"),
        check_vma=False,
    )
```

```python
import functools
import math

import jax
import jax.numpy as jnp
from jax import lax
from jax.experimental import pallas as pl
from jax.experimental.pallas import tpu as pltpu
from jax.sharding import PartitionSpec as P

MEMBERS = 256
OWN = 16
CELLS = 8192
OBS_W = 4096
HALO = 256
WIN = OBS_W + 2 * HALO
NPICK = 1024
ITERS = 6
N_WIDE = 16
N_NARROW = 16
LANES = 128
WIN_ROWS = WIN // LANES
CHUNKS = 8
CHUNK = CELLS // CHUNKS
TILE = 256
LEFT = 2560
VALUE_ROW, PREC_ROW, TAPER_ROW = 0, OBS_W // LANES, 2 * OBS_W // LANES
PICK_ROW = TAPER_ROW + NPICK // LANES
MESH = pl.DeviceIdType.MESH
HIGH = lax.Precision.HIGHEST
NT = (((1,), (1,)), ((), ()))

PEERS = [
    (1, 0, 0), (0, 1, 0), (3, 0, 1), (2, 1, 1), (1, 0, 1), (0, 1, 1), (3, 0, 0), (2, 0, 0),
    (1, 1, 0), (2, 0, 1), (3, 1, 1), (1, 1, 1), (2, 1, 0), (3, 1, 0), (0, 0, 1),
]


def kernel(states, obs, small, out,
           inbuf, outbuf, win, vwin, pwin, tapwin, gram, facc, trans,
           in_send, in_recv, out_send, out_recv, loc_sem, halo_send, halo_recv, obs_send, obs_recv):
    w = lax.axis_index("wide")
    n = lax.axis_index("narrow")
    y, x, c = n // 4, (n // 2) % 2, n % 2

    def at(dy, dx, dc):
        yy, xx, cc = (y + dy) % 4, (x + dx) % 2, (c + dc) % 2
        return 4 * yy + 2 * xx + cc, 4 * yy + 2 * cc + xx

    peers = [at(*d) for d in PEERS]
    before, after = (w + N_WIDE - 1) % N_WIDE, (w + 1) % N_WIDE
    me = 4 * y + 2 * c + x

    def rows(slot, count=1):
        return pl.ds(pl.multiple_of(slot * OWN, OWN), count * OWN)

    barrier = pltpu.get_barrier_semaphore()
    for index, _ in peers:
        pl.semaphore_signal(barrier, inc=1, device_id=(w, index), device_id_type=MESH)
    pl.semaphore_signal(barrier, inc=1, device_id=(before, n), device_id_type=MESH)

    mine = rows(me)
    win[mine, 0:OBS_W] = obs[...]
    vwin[0:32] = small[VALUE_ROW : VALUE_ROW + 32, :]
    pwin[0:32] = small[PREC_ROW : PREC_ROW + 32, :]
    own_states = pltpu.make_async_copy(
        states.at[:, pl.ds(pl.multiple_of(n * CELLS, CELLS), CELLS)], inbuf.at[mine], loc_sem.at[0]
    )
    own_states.start()
    pl.semaphore_wait(barrier, len(PEERS) + 1)

    def remote(src, dst, send, recv, device):
        return pltpu.make_async_remote_copy(
            src_ref=src, dst_ref=dst, send_sem=send, recv_sem=recv, device_id=device, device_id_type=MESH
        )

    halos = [
        remote(win.at[mine, pl.ds(OBS_W - HALO, HALO)], win.at[mine, pl.ds(OBS_W, HALO)],
               halo_send.at[0], halo_recv.at[0], (after, n)),
        remote(win.at[mine, pl.ds(0, HALO)], win.at[mine, pl.ds(OBS_W + HALO, HALO)],
               halo_send.at[1], halo_recv.at[1], (before, n)),
        remote(small.at[pl.ds(VALUE_ROW + 24, 8)], vwin.at[pl.ds(32, 8)], halo_send.at[2], halo_recv.at[2], (after, n)),
        remote(small.at[pl.ds(VALUE_ROW, 8)], vwin.at[pl.ds(40, 8)], halo_send.at[3], halo_recv.at[3], (before, n)),
        remote(small.at[pl.ds(PREC_ROW + 24, 8)], pwin.at[pl.ds(32, 8)], halo_send.at[4], halo_recv.at[4], (after, n)),
        remote(small.at[pl.ds(PREC_ROW, 8)], pwin.at[pl.ds(40, 8)], halo_send.at[5], halo_recv.at[5], (before, n)),
    ]
    for copy in halos[0::2]:
        copy.start()

    def send_states(chunk):
        for index, _ in peers:
            start = pl.multiple_of(index * CELLS + chunk * CHUNK, CHUNK)
            remote(states.at[:, pl.ds(start, CHUNK)],
                   inbuf.at[mine, pl.ds(pl.multiple_of(chunk * CHUNK, CHUNK), CHUNK)],
                   in_send.at[chunk], in_recv.at[chunk], (w, index)).start()

    left, right = (0, LEFT), (LEFT, WIN - LEFT)
    half = (WIN - LEFT) // 2
    right_low, right_high = (LEFT, half), (LEFT + half, half)
    moves = []

    def move(slot, count, columns, to):
        sem = len(moves)
        block = win.at[rows(slot, count), pl.ds(*columns)]
        copy = remote(block, block, obs_send.at[sem], obs_recv.at[sem], (w, at(*to)[0]))
        copy.start()
        moves.append(copy)
        return copy

    def pair(dy):
        return 4 * ((y + dy) % 4) + 2 * c

    def one(dy):
        return pair(dy) + x

    up, down, across, core = (1, 0, 0), (3, 0, 0), (0, 1, 0), (0, 0, 1)
    left_x = move(one(0), 1, left, across)
    send_states(0)
    left_x.wait_recv()
    left_up = move(pair(0), 2, left, up)
    left_down = move(pair(0), 2, left, down)
    last = [move(pair(0), 2, left, core)]
    halos[0].wait_recv()
    for copy in halos[1::2]:
        copy.start()
    send_states(1)
    halos[1].wait_recv()
    right_up = move(one(0), 1, right, up)
    right_down = move(one(0), 1, right, down)
    right_x0 = move(one(0), 1, right, across)
    left_up.wait_recv()
    left_up2 = move(pair(3), 1, left, up)
    last.append(move(pair(3), 2, left, core))
    left_down.wait_recv()
    left_down2 = move(pair(1) + 1, 1, left, down)
    last.append(move(pair(1), 2, left, core))
    send_states(2)
    right_up.wait_recv()
    right_up2 = move(one(3), 1, right_low, up)
    right_x3 = move(one(3), 1, right, across)
    right_down.wait_recv()
    right_down2 = move(one(1), 1, right_high, down)
    right_x1 = move(one(1), 1, right, across)
    left_up2.wait_recv()
    left_down2.wait_recv()
    last.append(move(pair(2), 2, left, core))
    send_states(3)
    right_up2.wait_recv()
    right_down2.wait_recv()
    right_x2 = move(one(2), 1, right, across)
    right_x0.wait_recv()
    last.append(move(pair(0), 2, right, core))
    right_x3.wait_recv()
    last.append(move(pair(3), 2, right, core))
    right_x1.wait_recv()
    last.append(move(pair(1), 2, right, core))
    send_states(4)
    right_x2.wait_recv()
    last.append(move(pair(2), 2, right, core))

    @pl.loop(5, CHUNKS)
    def _(chunk):
        send_states(chunk)

    own_taper = jnp.concatenate([small[TAPER_ROW + k : TAPER_ROW + k + 1, :] for k in range(8)], axis=1)
    own_pick = jnp.concatenate([small[PICK_ROW + k : PICK_ROW + k + 1, :] for k in range(8)], axis=1).astype(jnp.int32)
    own_pick = jnp.where(
        own_pick < HALO, own_pick + OBS_W, jnp.where(own_pick < HALO + OBS_W, own_pick - HALO, own_pick)
    )
    coarse = lax.broadcasted_iota(jnp.int32, (40, NPICK), 0) == (own_pick >> 7)
    fine = lax.broadcasted_iota(jnp.int32, (LANES, NPICK), 0) == (own_pick & 127)
    tapwin[...] = lax.dot_general(
        jnp.where(coarse, own_taper, 0.0), fine.astype(jnp.float32), NT,
        precision=HIGH, preferred_element_type=jnp.float32,
    )
    gram[...] = jnp.zeros_like(gram)
    facc[...] = jnp.zeros_like(facc)
    for copy in halos[2:]:
        copy.wait_recv()
    for copy in last:
        copy.wait_recv()

    @pl.loop(0, WIN // TILE)
    def _(tile):
        columns = pl.ds(pl.multiple_of(tile * TILE, TILE), TILE)

        def flat(ref, first):
            row = 2 * tile + first * (tile // (OBS_W // TILE))
            return jnp.concatenate([ref[pl.ds(row, 1), :], ref[pl.ds(row + 1, 1), :]], axis=1)

        ensemble = win[:, columns].astype(jnp.float32)
        mean = jnp.sum(ensemble, axis=0, keepdims=True) * (1.0 / MEMBERS)
        pert = ensemble - mean
        weight = flat(pwin, 6) * flat(tapwin, 0)
        scaled = (pert * jnp.sqrt(weight)).astype(jnp.bfloat16)
        gram[...] += lax.dot_general(scaled, scaled, NT, preferred_element_type=jnp.float32)
        force = pert * (weight * (flat(vwin, 6) - mean))
        facc[...] += force[:, :LANES] + force[:, LANES:]

    identity = (
        lax.broadcasted_iota(jnp.int32, (MEMBERS, MEMBERS), 0)
        == lax.broadcasted_iota(jnp.int32, (MEMBERS, MEMBERS), 1)
    ).astype(jnp.float32)

    def dot(a, b):
        return jnp.dot(a, b, precision=HIGH, preferred_element_type=jnp.float32)

    matrix = gram[...] + (MEMBERS - 1.0) * identity
    scale = jnp.sqrt(jnp.sum(jnp.sum(matrix * matrix, axis=0, keepdims=True), axis=1, keepdims=True))
    start = matrix / scale
    first = 1.5 * identity - 0.5 * start
    gram[...] = dot(start, first)
    trans[...] = first

    @pl.loop(0, ITERS - 2)
    def _(_):
        current, root = gram[...], trans[...]
        middle = 1.5 * identity - 0.5 * dot(root, current)
        gram[...] = dot(current, middle)
        trans[...] = dot(middle, root)

    root = dot(1.5 * identity - 0.5 * dot(trans[...], gram[...]), trans[...])
    inv_root = root / jnp.sqrt(scale)
    force = lax.dot_general(
        jnp.ones((8, LANES), jnp.float32), facc[...], NT, precision=HIGH, preferred_element_type=jnp.float32
    )
    inner = lax.dot_general(force, inv_root, NT, precision=HIGH, preferred_element_type=jnp.float32)
    weights = lax.dot_general(inner, inv_root, NT, precision=HIGH, preferred_element_type=jnp.float32)
    transform = (math.sqrt(MEMBERS - 1.0) * inv_root + weights[0:1]).astype(jnp.bfloat16)
    trans[...] = transform.astype(jnp.float32)
    own_states.wait()

    @pl.loop(0, CHUNKS)
    def _(chunk):
        columns = pl.ds(pl.multiple_of(chunk * CHUNK, CHUNK), CHUNK)
        arrived = inbuf.at[pl.ds(0, MEMBERS - OWN), columns]
        pltpu.make_async_copy(arrived, arrived, in_recv.at[chunk]).wait()
        mixer = trans[...].astype(jnp.bfloat16)

        @pl.loop(0, CHUNK // TILE)
        def _(tile):
            part = pl.ds(pl.multiple_of(chunk * CHUNK + tile * TILE, TILE), TILE)
            entries = inbuf[:, part].astype(jnp.float32)
            mean = jnp.sum(entries, axis=0, keepdims=True) * (1.0 / MEMBERS)
            pert = (entries - mean).astype(jnp.bfloat16)
            mixed = jnp.dot(mixer, pert, preferred_element_type=jnp.float32)
            outbuf[:, part] = (mean + mixed).astype(jnp.bfloat16)

        target = pl.ds(pl.multiple_of(n * CELLS + chunk * CHUNK, CHUNK), CHUNK)
        for index, slot in peers:
            remote(outbuf.at[rows(slot), columns], out.at[:, target],
                   out_send.at[chunk], out_recv.at[chunk], (w, index)).start()

    own_out = pltpu.make_async_copy(
        outbuf.at[mine], out.at[:, pl.ds(pl.multiple_of(n * CELLS, CELLS), CELLS)], loc_sem.at[1]
    )
    own_out.start()
    for copy in halos:
        copy.wait_send()
    for copy in moves:
        copy.wait_send()

    @pl.loop(0, CHUNKS)
    def _(chunk):
        columns = pl.ds(pl.multiple_of(chunk * CHUNK, CHUNK), CHUNK)
        most = outbuf.at[pl.ds(0, MEMBERS - OWN), columns]
        pltpu.make_async_copy(most, most, in_send.at[chunk]).wait()
        pltpu.make_async_copy(most, most, out_send.at[chunk]).wait()
        pltpu.make_async_copy(most, most, out_recv.at[chunk]).wait()

    own_out.wait()


def body(states, obs_ens, obs_value, obs_prec, obs_pick, taper):
    vmem, anywhere = (pl.BlockSpec(memory_space=pltpu.VMEM), pl.BlockSpec(memory_space=pl.ANY))
    dma = pltpu.SemaphoreType.DMA

    own_pick = lax.dynamic_slice_in_dim(obs_pick, lax.axis_index("narrow"), 1, 0)
    small = jnp.concatenate(
        [part.astype(jnp.float32).reshape(-1, LANES) for part in (obs_value, obs_prec, taper, own_pick)], axis=0
    )
    return pl.pallas_call(
        kernel,
        out_shape=jax.ShapeDtypeStruct(states.shape, jnp.bfloat16),
        in_specs=[anywhere, vmem, vmem],
        out_specs=anywhere,
        scratch_shapes=[
            pltpu.VMEM((MEMBERS, CELLS), jnp.bfloat16),
            pltpu.VMEM((MEMBERS, CELLS), jnp.bfloat16),
            pltpu.VMEM((MEMBERS, WIN), jnp.bfloat16),
            pltpu.VMEM((48, LANES), jnp.float32),
            pltpu.VMEM((48, LANES), jnp.float32),
            pltpu.VMEM((40, LANES), jnp.float32),
            pltpu.VMEM((MEMBERS, MEMBERS), jnp.float32),
            pltpu.VMEM((MEMBERS, LANES), jnp.float32),
            pltpu.VMEM((MEMBERS, MEMBERS), jnp.float32),
            dma((CHUNKS,)),
            dma((CHUNKS,)),
            dma((CHUNKS,)),
            dma((CHUNKS,)),
            dma((2,)),
            dma((6,)),
            dma((6,)),
            dma((21,)),
            dma((21,)),
        ],
        compiler_params=pltpu.CompilerParams(
            collective_id=0, has_side_effects=True, vmem_limit_bytes=48 << 20
        ),
        name="analysis",
    )(states, obs_ens, small)


def solution(mesh):
    return jax.shard_map(
        body,
        mesh=mesh,
        in_specs=(
            P("narrow", "wide"),
            P("narrow", "wide"),
            P("wide"),
            P("wide"),
            P("wide", None),
            P(("wide", "narrow"), None),
        ),
        out_specs=P("narrow", "wide"),
        check_vma=False,
    )
```

```python
import math

import jax
import jax.numpy as jnp
from jax import lax
from jax.experimental import pallas as pl
from jax.experimental.pallas import tpu as pltpu
from jax.sharding import PartitionSpec as P

MEMBERS = 256
OWN = 16
CELLS = 8192
OBS_W = 4096
HALO = 256
WIN = OBS_W + 2 * HALO
NPICK = 1024
ITERS = 6
N_WIDE = 16
LANES = 128
CHUNKS = 8
CHUNK = CELLS // CHUNKS
TILE = 256
LEFT = 2560
MESH = pl.DeviceIdType.MESH
HIGH = lax.Precision.HIGHEST
NT = (((1,), (1,)), ((), ()))

PEERS = [
    (1, 0, 0), (0, 1, 0), (3, 0, 1), (2, 1, 1), (1, 0, 1), (0, 1, 1), (3, 0, 0), (2, 0, 0),
    (1, 1, 0), (2, 0, 1), (3, 1, 1), (1, 1, 1), (2, 1, 0), (3, 1, 0), (0, 0, 1),
]


def kernel(states, obs, value, prec, pick, taper, out,
           inbuf, outbuf, win, vwin, pwin, picked, tap, tapwin, gram, facc, trans,
           in_send, in_recv, out_send, out_recv, loc_sem, halo_send, halo_recv, obs_send, obs_recv):
    w = lax.axis_index("wide")
    n = lax.axis_index("narrow")
    y, x, c = n // 4, (n // 2) % 2, n % 2

    def at(dy, dx, dc):
        yy, xx, cc = (y + dy) % 4, (x + dx) % 2, (c + dc) % 2
        return 4 * yy + 2 * xx + cc, 4 * yy + 2 * cc + xx

    peers = [at(*d) for d in PEERS]
    before, after = (w + N_WIDE - 1) % N_WIDE, (w + 1) % N_WIDE
    me = 4 * y + 2 * c + x

    def rows(slot, count=1):
        return pl.ds(pl.multiple_of(slot * OWN, OWN), count * OWN)

    barrier = pltpu.get_barrier_semaphore()
    for index, _ in peers:
        pl.semaphore_signal(barrier, inc=1, device_id=(w, index), device_id_type=MESH)
    pl.semaphore_signal(barrier, inc=1, device_id=(before, n), device_id_type=MESH)

    mine = rows(me)
    locals_ = [
        pltpu.make_async_copy(obs, win.at[mine, pl.ds(0, OBS_W)], loc_sem.at[2]),
        pltpu.make_async_copy(value, vwin.at[pl.ds(0, 32)], loc_sem.at[3]),
        pltpu.make_async_copy(prec, pwin.at[pl.ds(0, 32)], loc_sem.at[4]),
        pltpu.make_async_copy(pick.at[pl.ds(pl.multiple_of(n // 8 * 8, 8), 8)], picked, loc_sem.at[5]),
        pltpu.make_async_copy(taper, tap, loc_sem.at[6]),
    ]
    for copy in locals_:
        copy.start()
    own_states = pltpu.make_async_copy(
        states.at[:, pl.ds(pl.multiple_of(n * CELLS, CELLS), CELLS)], inbuf.at[mine], loc_sem.at[0]
    )
    own_states.start()
    pl.semaphore_wait(barrier, len(PEERS) + 1)

    def remote(src, dst, send, recv, device):
        return pltpu.make_async_remote_copy(
            src_ref=src, dst_ref=dst, send_sem=send, recv_sem=recv, device_id=device, device_id_type=MESH
        )

    halos = [
        remote(obs.at[:, pl.ds(OBS_W - HALO, HALO)], win.at[mine, pl.ds(OBS_W, HALO)],
               halo_send.at[0], halo_recv.at[0], (after, n)),
        remote(obs.at[:, pl.ds(0, HALO)], win.at[mine, pl.ds(OBS_W + HALO, HALO)],
               halo_send.at[1], halo_recv.at[1], (before, n)),
        remote(value.at[pl.ds(24, 8)], vwin.at[pl.ds(32, 8)], halo_send.at[2], halo_recv.at[2], (after, n)),
        remote(value.at[pl.ds(0, 8)], vwin.at[pl.ds(40, 8)], halo_send.at[3], halo_recv.at[3], (before, n)),
        remote(prec.at[pl.ds(24, 8)], pwin.at[pl.ds(32, 8)], halo_send.at[4], halo_recv.at[4], (after, n)),
        remote(prec.at[pl.ds(0, 8)], pwin.at[pl.ds(40, 8)], halo_send.at[5], halo_recv.at[5], (before, n)),
    ]
    for copy in halos[0::2]:
        copy.start()

    def send_states(chunk):
        for index, _ in peers:
            start = pl.multiple_of(index * CELLS + chunk * CHUNK, CHUNK)
            remote(states.at[:, pl.ds(start, CHUNK)],
                   inbuf.at[mine, pl.ds(pl.multiple_of(chunk * CHUNK, CHUNK), CHUNK)],
                   in_send.at[chunk], in_recv.at[chunk], (w, index)).start()

    left, right = (0, LEFT), (LEFT, WIN - LEFT)
    half = (WIN - LEFT) // 2
    right_low, right_high = (LEFT, half), (LEFT + half, half)
    moves = []

    def move(slot, count, columns, to):
        sem = len(moves)
        block = win.at[rows(slot, count), pl.ds(*columns)]
        copy = remote(block, block, obs_send.at[sem], obs_recv.at[sem], (w, at(*to)[0]))
        copy.start()
        moves.append(copy)
        return copy

    def pair(dy):
        return 4 * ((y + dy) % 4) + 2 * c

    def one(dy):
        return pair(dy) + x

    up, down, across, core = (1, 0, 0), (3, 0, 0), (0, 1, 0), (0, 0, 1)
    locals_[0].wait()
    left_x = move(one(0), 1, left, across)
    send_states(0)
    left_x.wait_recv()
    left_up = move(pair(0), 2, left, up)
    left_down = move(pair(0), 2, left, down)
    last = [move(pair(0), 2, left, core)]
    halos[0].wait_recv()
    for copy in halos[1::2]:
        copy.start()
    send_states(1)
    halos[1].wait_recv()
    right_up = move(one(0), 1, right, up)
    right_down = move(one(0), 1, right, down)
    right_x0 = move(one(0), 1, right, across)
    left_up.wait_recv()
    left_up2 = move(pair(3), 1, left, up)
    last.append(move(pair(3), 2, left, core))
    left_down.wait_recv()
    left_down2 = move(pair(1) + 1, 1, left, down)
    last.append(move(pair(1), 2, left, core))
    send_states(2)
    right_up.wait_recv()
    right_up2 = move(one(3), 1, right_low, up)
    right_x3 = move(one(3), 1, right, across)
    right_down.wait_recv()
    right_down2 = move(one(1), 1, right_high, down)
    right_x1 = move(one(1), 1, right, across)
    left_up2.wait_recv()
    left_down2.wait_recv()
    last.append(move(pair(2), 2, left, core))
    send_states(3)
    right_up2.wait_recv()
    right_down2.wait_recv()
    right_x2 = move(one(2), 1, right, across)
    right_x0.wait_recv()
    last.append(move(pair(0), 2, right, core))
    right_x3.wait_recv()
    last.append(move(pair(3), 2, right, core))
    right_x1.wait_recv()
    last.append(move(pair(1), 2, right, core))
    send_states(4)
    right_x2.wait_recv()
    last.append(move(pair(2), 2, right, core))

    @pl.loop(5, CHUNKS)
    def _(chunk):
        send_states(chunk)

    for copy in locals_[1:]:
        copy.wait()
    own_pick = picked[pl.ds(n % 8, 1), :]
    own_pick = jnp.where(
        own_pick < HALO, own_pick + OBS_W, jnp.where(own_pick < HALO + OBS_W, own_pick - HALO, own_pick)
    )
    coarse = lax.broadcasted_iota(jnp.int32, (40, NPICK), 0) == (own_pick >> 7)
    fine = lax.broadcasted_iota(jnp.int32, (LANES, NPICK), 0) == (own_pick & 127)
    tapwin[...] = lax.dot_general(
        jnp.where(coarse, tap[...], 0.0), fine.astype(jnp.float32), NT,
        precision=HIGH, preferred_element_type=jnp.float32,
    )
    gram[...] = jnp.zeros_like(gram)
    facc[...] = jnp.zeros_like(facc)
    for copy in halos[2:]:
        copy.wait_recv()
    for copy in last:
        copy.wait_recv()

    @pl.loop(0, WIN // TILE)
    def _(tile):
        columns = pl.ds(pl.multiple_of(tile * TILE, TILE), TILE)

        def flat(ref, first):
            row = 2 * tile + first * (tile // (OBS_W // TILE))
            return jnp.concatenate([ref[pl.ds(row, 1), :], ref[pl.ds(row + 1, 1), :]], axis=1)

        ensemble = win[:, columns].astype(jnp.float32)
        mean = jnp.sum(ensemble, axis=0, keepdims=True) * (1.0 / MEMBERS)
        pert = ensemble - mean
        weight = flat(pwin, 6) * flat(tapwin, 0)
        scaled = (pert * jnp.sqrt(weight)).astype(jnp.bfloat16)
        gram[...] += lax.dot_general(scaled, scaled, NT, preferred_element_type=jnp.float32)
        force = pert * (weight * (flat(vwin, 6) - mean))
        facc[...] += force[:, :LANES] + force[:, LANES:]

    identity = (
        lax.broadcasted_iota(jnp.int32, (MEMBERS, MEMBERS), 0)
        == lax.broadcasted_iota(jnp.int32, (MEMBERS, MEMBERS), 1)
    ).astype(jnp.float32)

    def dot(a, b):
        return jnp.dot(a, b, precision=HIGH, preferred_element_type=jnp.float32)

    matrix = gram[...] + (MEMBERS - 1.0) * identity
    scale = jnp.sqrt(jnp.sum(jnp.sum(matrix * matrix, axis=0, keepdims=True), axis=1, keepdims=True))
    start = matrix / scale
    first = 1.5 * identity - 0.5 * start
    gram[...] = dot(start, first)
    trans[...] = first

    @pl.loop(0, ITERS - 2)
    def _(_):
        current, root = gram[...], trans[...]
        middle = 1.5 * identity - 0.5 * dot(root, current)
        gram[...] = dot(current, middle)
        trans[...] = dot(middle, root)

    root = dot(1.5 * identity - 0.5 * dot(trans[...], gram[...]), trans[...])
    inv_root = root / jnp.sqrt(scale)
    force = lax.dot_general(
        jnp.ones((8, LANES), jnp.float32), facc[...], NT, precision=HIGH, preferred_element_type=jnp.float32
    )
    inner = lax.dot_general(force, inv_root, NT, precision=HIGH, preferred_element_type=jnp.float32)
    weights = lax.dot_general(inner, inv_root, NT, precision=HIGH, preferred_element_type=jnp.float32)
    transform = (math.sqrt(MEMBERS - 1.0) * inv_root + weights[0:1]).astype(jnp.bfloat16)
    trans[...] = transform.astype(jnp.float32)
    own_states.wait()

    @pl.loop(0, CHUNKS)
    def _(chunk):
        columns = pl.ds(pl.multiple_of(chunk * CHUNK, CHUNK), CHUNK)
        arrived = inbuf.at[pl.ds(0, MEMBERS - OWN), columns]
        pltpu.make_async_copy(arrived, arrived, in_recv.at[chunk]).wait()
        mixer = trans[...].astype(jnp.bfloat16)

        @pl.loop(0, CHUNK // TILE)
        def _(tile):
            part = pl.ds(pl.multiple_of(chunk * CHUNK + tile * TILE, TILE), TILE)
            entries = inbuf[:, part].astype(jnp.float32)
            mean = jnp.sum(entries, axis=0, keepdims=True) * (1.0 / MEMBERS)
            pert = (entries - mean).astype(jnp.bfloat16)
            mixed = jnp.dot(mixer, pert, preferred_element_type=jnp.float32)
            outbuf[:, part] = (mean + mixed).astype(jnp.bfloat16)

        target = pl.ds(pl.multiple_of(n * CELLS + chunk * CHUNK, CHUNK), CHUNK)
        for index, slot in peers:
            remote(outbuf.at[rows(slot), columns], out.at[:, target],
                   out_send.at[chunk], out_recv.at[chunk], (w, index)).start()

    own_out = pltpu.make_async_copy(
        outbuf.at[mine], out.at[:, pl.ds(pl.multiple_of(n * CELLS, CELLS), CELLS)], loc_sem.at[1]
    )
    own_out.start()
    for copy in halos:
        copy.wait_send()
    for copy in moves:
        copy.wait_send()

    @pl.loop(0, CHUNKS)
    def _(chunk):
        columns = pl.ds(pl.multiple_of(chunk * CHUNK, CHUNK), CHUNK)
        most = outbuf.at[pl.ds(0, MEMBERS - OWN), columns]
        pltpu.make_async_copy(most, most, in_send.at[chunk]).wait()
        pltpu.make_async_copy(most, most, out_send.at[chunk]).wait()
        pltpu.make_async_copy(most, most, out_recv.at[chunk]).wait()

    own_out.wait()


def body(states, obs_ens, obs_value, obs_prec, obs_pick, taper):
    anywhere = pl.BlockSpec(memory_space=pl.ANY)
    dma = pltpu.SemaphoreType.DMA

    return pl.pallas_call(
        kernel,
        out_shape=jax.ShapeDtypeStruct(states.shape, jnp.bfloat16),
        in_specs=[anywhere] * 6,
        out_specs=anywhere,
        scratch_shapes=[
            pltpu.VMEM((MEMBERS, CELLS), jnp.bfloat16),
            pltpu.VMEM((MEMBERS, CELLS), jnp.bfloat16),
            pltpu.VMEM((MEMBERS, WIN), jnp.bfloat16),
            pltpu.VMEM((48, LANES), jnp.float32),
            pltpu.VMEM((48, LANES), jnp.float32),
            pltpu.VMEM((8, NPICK), jnp.int32),
            pltpu.VMEM((1, NPICK), jnp.float32),
            pltpu.VMEM((40, LANES), jnp.float32),
            pltpu.VMEM((MEMBERS, MEMBERS), jnp.float32),
            pltpu.VMEM((MEMBERS, LANES), jnp.float32),
            pltpu.VMEM((MEMBERS, MEMBERS), jnp.float32),
            dma((CHUNKS,)),
            dma((CHUNKS,)),
            dma((CHUNKS,)),
            dma((CHUNKS,)),
            dma((7,)),
            dma((6,)),
            dma((6,)),
            dma((21,)),
            dma((21,)),
        ],
        compiler_params=pltpu.CompilerParams(
            collective_id=0, has_side_effects=True, vmem_limit_bytes=48 << 20
        ),
        name="analysis",
    )(*(pltpu.with_memory_space_constraint(a, pltpu.HBM) for a in (
        states,
        obs_ens,
        obs_value.reshape(OBS_W // LANES, LANES),
        obs_prec.reshape(OBS_W // LANES, LANES),
        obs_pick,
        taper,
    )))


def solution(mesh):
    return jax.shard_map(
        body,
        mesh=mesh,
        in_specs=(
            P("narrow", "wide"),
            P("narrow", "wide"),
            P("wide"),
            P("wide"),
            P("wide", None),
            P(("wide", "narrow"), None),
        ),
        out_specs=P("narrow", "wide"),
        check_vma=False,
    )
```

```python
import math

import jax
import jax.numpy as jnp
from jax import lax
from jax.experimental import pallas as pl
from jax.experimental.pallas import tpu as pltpu
from jax.sharding import PartitionSpec as P

MEMBERS = 256
OWN = 16
CELLS = 8192
OBS_W = 4096
HALO = 256
WIN = OBS_W + 2 * HALO
NPICK = 1024
ITERS = 6
N_WIDE = 16
LANES = 128
CHUNKS = 8
CHUNK = CELLS // CHUNKS
TILE = 256
LEFT = 2560
MESH = pl.DeviceIdType.MESH
HIGH = lax.Precision.HIGHEST
NT = (((1,), (1,)), ((), ()))

PEERS = [
    (1, 0, 0), (0, 1, 0), (3, 0, 1), (2, 1, 1), (1, 0, 1), (0, 1, 1), (3, 0, 0), (2, 0, 0),
    (1, 1, 0), (2, 0, 1), (3, 1, 1), (1, 1, 1), (2, 1, 0), (3, 1, 0), (0, 0, 1),
]


def kernel(states, obs, value, prec, pick, taper, out,
           inbuf, outbuf, win, vwin, pwin, picked, tap, tapwin, gram, facc, trans,
           in_send, in_recv, out_send, out_recv, loc_sem, halo_send, halo_recv, obs_send, obs_recv):
    w = lax.axis_index("wide")
    n = lax.axis_index("narrow")
    y, x, c = n // 4, (n // 2) % 2, n % 2

    def at(dy, dx, dc):
        yy, xx, cc = (y + dy) % 4, (x + dx) % 2, (c + dc) % 2
        return 4 * yy + 2 * xx + cc, 4 * yy + 2 * cc + xx

    peers = [at(*d) for d in PEERS]
    before, after = (w + N_WIDE - 1) % N_WIDE, (w + 1) % N_WIDE
    me = 4 * y + 2 * c + x

    def rows(slot, count=1):
        return pl.ds(pl.multiple_of(slot * OWN, OWN), count * OWN)

    barrier = pltpu.get_barrier_semaphore()
    for index, _ in peers:
        pl.semaphore_signal(barrier, inc=1, device_id=(w, index), device_id_type=MESH)
    first_band, last_band = w == 0, w == N_WIDE - 1

    @pl.when(jnp.logical_not(last_band))
    def _():
        pl.semaphore_signal(barrier, inc=1, device_id=(after, n), device_id_type=MESH)

    @pl.when(first_band)
    def _():
        pl.semaphore_signal(barrier, inc=1, device_id=(before, n), device_id_type=MESH)


    mine = rows(me)
    locals_ = [
        pltpu.make_async_copy(obs, win.at[mine, pl.ds(0, OBS_W)], loc_sem.at[2]),
        pltpu.make_async_copy(value, vwin.at[pl.ds(0, 32)], loc_sem.at[3]),
        pltpu.make_async_copy(prec, pwin.at[pl.ds(0, 32)], loc_sem.at[4]),
        pltpu.make_async_copy(pick.at[pl.ds(pl.multiple_of(n // 8 * 8, 8), 8)], picked, loc_sem.at[5]),
        pltpu.make_async_copy(taper, tap, loc_sem.at[6]),
    ]
    for copy in locals_:
        copy.start()
    own_states = pltpu.make_async_copy(
        states.at[:, pl.ds(pl.multiple_of(n * CELLS, CELLS), CELLS)], inbuf.at[mine], loc_sem.at[0]
    )
    own_states.start()
    pl.semaphore_wait(barrier, len(PEERS) + jnp.where(first_band, 0, jnp.where(last_band, 2, 1)))

    def remote(src, dst, send, recv, device):
        return pltpu.make_async_remote_copy(
            src_ref=src, dst_ref=dst, send_sem=send, recv_sem=recv, device_id=device, device_id_type=MESH
        )

    halos = [
        remote(obs.at[:, pl.ds(OBS_W - HALO, HALO)], win.at[mine, pl.ds(OBS_W, HALO)],
               halo_send.at[0], halo_recv.at[0], (after, n)),
        remote(obs.at[:, pl.ds(0, HALO)], win.at[mine, pl.ds(OBS_W + HALO, HALO)],
               halo_send.at[1], halo_recv.at[1], (before, n)),
        remote(value.at[pl.ds(24, 8)], vwin.at[pl.ds(32, 8)], halo_send.at[2], halo_recv.at[2], (after, n)),
        remote(value.at[pl.ds(0, 8)], vwin.at[pl.ds(40, 8)], halo_send.at[3], halo_recv.at[3], (before, n)),
        remote(prec.at[pl.ds(24, 8)], pwin.at[pl.ds(32, 8)], halo_send.at[4], halo_recv.at[4], (after, n)),
        remote(prec.at[pl.ds(0, 8)], pwin.at[pl.ds(40, 8)], halo_send.at[5], halo_recv.at[5], (before, n)),
    ]
    to_after, to_before = halos[0::2], halos[1::2]

    def start_if(condition, copies):
        @pl.when(condition)
        def _():
            for copy in copies:
                copy.start()

    start_if(jnp.logical_not(first_band), to_before)
    start_if(last_band, to_after)

    def send_states(chunk):
        for index, _ in peers:
            start = pl.multiple_of(index * CELLS + chunk * CHUNK, CHUNK)
            remote(states.at[:, pl.ds(start, CHUNK)],
                   inbuf.at[mine, pl.ds(pl.multiple_of(chunk * CHUNK, CHUNK), CHUNK)],
                   in_send.at[chunk], in_recv.at[chunk], (w, index)).start()

    left, right = (0, LEFT), (LEFT, WIN - LEFT)
    half = (WIN - LEFT) // 2
    right_low, right_high = (LEFT, half), (LEFT + half, half)
    moves = []

    def move(slot, count, columns, to):
        sem = len(moves)
        block = win.at[rows(slot, count), pl.ds(*columns)]
        copy = remote(block, block, obs_send.at[sem], obs_recv.at[sem], (w, at(*to)[0]))
        copy.start()
        moves.append(copy)
        return copy

    def pair(dy):
        return 4 * ((y + dy) % 4) + 2 * c

    def one(dy):
        return pair(dy) + x

    up, down, across, core = (1, 0, 0), (3, 0, 0), (0, 1, 0), (0, 0, 1)
    locals_[0].wait()
    left_x = move(one(0), 1, left, across)
    send_states(0)
    left_x.wait_recv()
    left_up = move(pair(0), 2, left, up)
    left_down = move(pair(0), 2, left, down)
    last = [move(pair(0), 2, left, core)]
    halos[1].wait_recv()
    start_if(jnp.logical_not(last_band), to_after)
    send_states(1)
    halos[0].wait_recv()
    start_if(first_band, to_before)
    right_up = move(one(0), 1, right, up)
    right_down = move(one(0), 1, right, down)
    right_x0 = move(one(0), 1, right, across)
    left_up.wait_recv()
    left_up2 = move(pair(3), 1, left, up)
    last.append(move(pair(3), 2, left, core))
    left_down.wait_recv()
    left_down2 = move(pair(1) + 1, 1, left, down)
    last.append(move(pair(1), 2, left, core))
    send_states(2)
    right_up.wait_recv()
    right_up2 = move(one(3), 1, right_low, up)
    right_x3 = move(one(3), 1, right, across)
    right_down.wait_recv()
    right_down2 = move(one(1), 1, right_high, down)
    right_x1 = move(one(1), 1, right, across)
    left_up2.wait_recv()
    left_down2.wait_recv()
    last.append(move(pair(2), 2, left, core))
    send_states(3)
    right_up2.wait_recv()
    right_down2.wait_recv()
    right_x2 = move(one(2), 1, right, across)
    right_x0.wait_recv()
    last.append(move(pair(0), 2, right, core))
    right_x3.wait_recv()
    last.append(move(pair(3), 2, right, core))
    right_x1.wait_recv()
    last.append(move(pair(1), 2, right, core))
    send_states(4)
    right_x2.wait_recv()
    last.append(move(pair(2), 2, right, core))

    @pl.loop(5, CHUNKS)
    def _(chunk):
        send_states(chunk)

    for copy in locals_[1:]:
        copy.wait()
    own_pick = picked[pl.ds(n % 8, 1), :]
    own_pick = jnp.where(
        own_pick < HALO, own_pick + OBS_W, jnp.where(own_pick < HALO + OBS_W, own_pick - HALO, own_pick)
    )
    coarse = lax.broadcasted_iota(jnp.int32, (40, NPICK), 0) == (own_pick >> 7)
    fine = lax.broadcasted_iota(jnp.int32, (LANES, NPICK), 0) == (own_pick & 127)
    tapwin[...] = lax.dot_general(
        jnp.where(coarse, tap[...], 0.0), fine.astype(jnp.float32), NT,
        precision=HIGH, preferred_element_type=jnp.float32,
    )
    gram[...] = jnp.zeros_like(gram)
    facc[...] = jnp.zeros_like(facc)
    for copy in halos[2:]:
        copy.wait_recv()
    for copy in last:
        copy.wait_recv()

    @pl.loop(0, WIN // TILE)
    def _(tile):
        columns = pl.ds(pl.multiple_of(tile * TILE, TILE), TILE)

        def flat(ref, first):
            row = 2 * tile + first * (tile // (OBS_W // TILE))
            return jnp.concatenate([ref[pl.ds(row, 1), :], ref[pl.ds(row + 1, 1), :]], axis=1)

        ensemble = win[:, columns].astype(jnp.float32)
        mean = jnp.sum(ensemble, axis=0, keepdims=True) * (1.0 / MEMBERS)
        pert = ensemble - mean
        weight = flat(pwin, 6) * flat(tapwin, 0)
        scaled = (pert * jnp.sqrt(weight)).astype(jnp.bfloat16)
        gram[...] += lax.dot_general(scaled, scaled, NT, preferred_element_type=jnp.float32)
        force = pert * (weight * (flat(vwin, 6) - mean))
        facc[...] += force[:, :LANES] + force[:, LANES:]

    identity = (
        lax.broadcasted_iota(jnp.int32, (MEMBERS, MEMBERS), 0)
        == lax.broadcasted_iota(jnp.int32, (MEMBERS, MEMBERS), 1)
    ).astype(jnp.float32)

    def dot(a, b):
        return jnp.dot(a, b, precision=HIGH, preferred_element_type=jnp.float32)

    matrix = gram[...] + (MEMBERS - 1.0) * identity
    scale = jnp.sqrt(jnp.sum(jnp.sum(matrix * matrix, axis=0, keepdims=True), axis=1, keepdims=True))
    start = matrix / scale
    first = 1.5 * identity - 0.5 * start
    gram[...] = dot(start, first)
    trans[...] = first

    @pl.loop(0, ITERS - 2)
    def _(_):
        current, root = gram[...], trans[...]
        middle = 1.5 * identity - 0.5 * dot(root, current)
        gram[...] = dot(current, middle)
        trans[...] = dot(middle, root)

    root = dot(1.5 * identity - 0.5 * dot(trans[...], gram[...]), trans[...])
    inv_root = root / jnp.sqrt(scale)
    force = lax.dot_general(
        jnp.ones((8, LANES), jnp.float32), facc[...], NT, precision=HIGH, preferred_element_type=jnp.float32
    )
    inner = lax.dot_general(force, inv_root, NT, precision=HIGH, preferred_element_type=jnp.float32)
    weights = lax.dot_general(inner, inv_root, NT, precision=HIGH, preferred_element_type=jnp.float32)
    transform = (math.sqrt(MEMBERS - 1.0) * inv_root + weights[0:1]).astype(jnp.bfloat16)
    trans[...] = transform.astype(jnp.float32)
    own_states.wait()

    @pl.loop(0, CHUNKS)
    def _(chunk):
        columns = pl.ds(pl.multiple_of(chunk * CHUNK, CHUNK), CHUNK)
        arrived = inbuf.at[pl.ds(0, MEMBERS - OWN), columns]
        pltpu.make_async_copy(arrived, arrived, in_recv.at[chunk]).wait()
        mixer = trans[...].astype(jnp.bfloat16)

        @pl.loop(0, CHUNK // TILE)
        def _(tile):
            part = pl.ds(pl.multiple_of(chunk * CHUNK + tile * TILE, TILE), TILE)
            entries = inbuf[:, part].astype(jnp.float32)
            mean = jnp.sum(entries, axis=0, keepdims=True) * (1.0 / MEMBERS)
            pert = (entries - mean).astype(jnp.bfloat16)
            mixed = jnp.dot(mixer, pert, preferred_element_type=jnp.float32)
            outbuf[:, part] = (mean + mixed).astype(jnp.bfloat16)

        target = pl.ds(pl.multiple_of(n * CELLS + chunk * CHUNK, CHUNK), CHUNK)
        for index, slot in peers:
            remote(outbuf.at[rows(slot), columns], out.at[:, target],
                   out_send.at[chunk], out_recv.at[chunk], (w, index)).start()

    own_out = pltpu.make_async_copy(
        outbuf.at[mine], out.at[:, pl.ds(pl.multiple_of(n * CELLS, CELLS), CELLS)], loc_sem.at[1]
    )
    own_out.start()
    for copy in halos:
        copy.wait_send()
    for copy in moves:
        copy.wait_send()

    @pl.loop(0, CHUNKS)
    def _(chunk):
        columns = pl.ds(pl.multiple_of(chunk * CHUNK, CHUNK), CHUNK)
        most = outbuf.at[pl.ds(0, MEMBERS - OWN), columns]
        pltpu.make_async_copy(most, most, in_send.at[chunk]).wait()
        pltpu.make_async_copy(most, most, out_send.at[chunk]).wait()
        pltpu.make_async_copy(most, most, out_recv.at[chunk]).wait()

    own_out.wait()


def body(states, obs_ens, obs_value, obs_prec, obs_pick, taper):
    anywhere = pl.BlockSpec(memory_space=pl.ANY)
    dma = pltpu.SemaphoreType.DMA

    return pl.pallas_call(
        kernel,
        out_shape=jax.ShapeDtypeStruct(states.shape, jnp.bfloat16),
        in_specs=[anywhere] * 6,
        out_specs=anywhere,
        scratch_shapes=[
            pltpu.VMEM((MEMBERS, CELLS), jnp.bfloat16),
            pltpu.VMEM((MEMBERS, CELLS), jnp.bfloat16),
            pltpu.VMEM((MEMBERS, WIN), jnp.bfloat16),
            pltpu.VMEM((48, LANES), jnp.float32),
            pltpu.VMEM((48, LANES), jnp.float32),
            pltpu.VMEM((8, NPICK), jnp.int32),
            pltpu.VMEM((1, NPICK), jnp.float32),
            pltpu.VMEM((40, LANES), jnp.float32),
            pltpu.VMEM((MEMBERS, MEMBERS), jnp.float32),
            pltpu.VMEM((MEMBERS, LANES), jnp.float32),
            pltpu.VMEM((MEMBERS, MEMBERS), jnp.float32),
            dma((CHUNKS,)),
            dma((CHUNKS,)),
            dma((CHUNKS,)),
            dma((CHUNKS,)),
            dma((7,)),
            dma((6,)),
            dma((6,)),
            dma((21,)),
            dma((21,)),
        ],
        compiler_params=pltpu.CompilerParams(
            collective_id=0, has_side_effects=True, vmem_limit_bytes=48 << 20
        ),
        name="analysis",
    )(*(pltpu.with_memory_space_constraint(a, pltpu.HBM) for a in (
        states,
        obs_ens,
        obs_value.reshape(OBS_W // LANES, LANES),
        obs_prec.reshape(OBS_W // LANES, LANES),
        obs_pick,
        taper,
    )))


def solution(mesh):
    return jax.shard_map(
        body,
        mesh=mesh,
        in_specs=(
            P("narrow", "wide"),
            P("narrow", "wide"),
            P("wide"),
            P("wide"),
            P("wide", None),
            P(("wide", "narrow"), None),
        ),
        out_specs=P("narrow", "wide"),
        check_vma=False,
    )
```

```python
import math

import jax
import jax.numpy as jnp
from jax import lax
from jax.experimental import pallas as pl
from jax.experimental.pallas import tpu as pltpu
from jax.sharding import PartitionSpec as P

MEMBERS = 256
OWN = 16
CELLS = 8192
OBS_W = 4096
HALO = 256
WIN = OBS_W + 2 * HALO
NPICK = 1024
ITERS = 6
N_WIDE = 16
LANES = 128
CHUNKS = 8
CHUNK = CELLS // CHUNKS
TILE = 256
LEFT = 2560
MESH = pl.DeviceIdType.MESH
HIGH = lax.Precision.HIGHEST
NT = (((1,), (1,)), ((), ()))

PEERS = [
    (2, 0, 0), (1, 0, 0), (3, 0, 0), (2, 0, 1), (1, 0, 1), (3, 0, 1), (0, 0, 1), (2, 1, 0),
    (1, 1, 0), (3, 1, 0), (0, 1, 0), (2, 1, 1), (1, 1, 1), (3, 1, 1), (0, 1, 1),
]


def kernel(states, obs, value, prec, pick, taper, out,
           inbuf, outbuf, win, vwin, pwin, picked, tap, tapwin, gram, facc, trans,
           in_send, in_recv, out_send, out_recv, loc_sem, halo_send, halo_recv, obs_send, obs_recv):
    w = lax.axis_index("wide")
    n = lax.axis_index("narrow")
    y, x, c = n // 4, (n // 2) % 2, n % 2

    def at(dy, dx, dc):
        yy, xx, cc = (y + dy) % 4, (x + dx) % 2, (c + dc) % 2
        return 4 * yy + 2 * xx + cc, 4 * yy + 2 * cc + xx

    peers = [
        tuple(jnp.where(c == 0, first, second) for first, second in zip(at(*a), at(*b)))
        for a, b in zip(PEERS, PEERS[7:] + PEERS[:7])
    ]
    before, after = (w + N_WIDE - 1) % N_WIDE, (w + 1) % N_WIDE
    me = 4 * y + 2 * c + x

    def rows(slot, count=1):
        return pl.ds(pl.multiple_of(slot * OWN, OWN), count * OWN)

    barrier = pltpu.get_barrier_semaphore()
    for index, _ in peers:
        pl.semaphore_signal(barrier, inc=1, device_id=(w, index), device_id_type=MESH)
    first_band, last_band = w == 0, w == N_WIDE - 1

    @pl.when(jnp.logical_not(last_band))
    def _():
        pl.semaphore_signal(barrier, inc=1, device_id=(after, n), device_id_type=MESH)

    @pl.when(first_band)
    def _():
        pl.semaphore_signal(barrier, inc=1, device_id=(before, n), device_id_type=MESH)


    mine = rows(me)
    locals_ = [
        pltpu.make_async_copy(obs, win.at[mine, pl.ds(0, OBS_W)], loc_sem.at[2]),
        pltpu.make_async_copy(value, vwin.at[pl.ds(0, 32)], loc_sem.at[3]),
        pltpu.make_async_copy(prec, pwin.at[pl.ds(0, 32)], loc_sem.at[4]),
        pltpu.make_async_copy(pick.at[pl.ds(pl.multiple_of(n // 8 * 8, 8), 8)], picked, loc_sem.at[5]),
        pltpu.make_async_copy(taper, tap, loc_sem.at[6]),
    ]
    for copy in locals_:
        copy.start()
    own_states = pltpu.make_async_copy(
        states.at[:, pl.ds(pl.multiple_of(n * CELLS, CELLS), CELLS)], inbuf.at[mine], loc_sem.at[0]
    )
    own_states.start()
    pl.semaphore_wait(barrier, len(PEERS) + jnp.where(first_band, 0, jnp.where(last_band, 2, 1)))

    def remote(src, dst, send, recv, device):
        return pltpu.make_async_remote_copy(
            src_ref=src, dst_ref=dst, send_sem=send, recv_sem=recv, device_id=device, device_id_type=MESH
        )

    halos = [
        remote(obs.at[:, pl.ds(OBS_W - HALO, HALO)], win.at[mine, pl.ds(OBS_W, HALO)],
               halo_send.at[0], halo_recv.at[0], (after, n)),
        remote(obs.at[:, pl.ds(0, HALO)], win.at[mine, pl.ds(OBS_W + HALO, HALO)],
               halo_send.at[1], halo_recv.at[1], (before, n)),
        remote(value.at[pl.ds(24, 8)], vwin.at[pl.ds(32, 8)], halo_send.at[2], halo_recv.at[2], (after, n)),
        remote(value.at[pl.ds(0, 8)], vwin.at[pl.ds(40, 8)], halo_send.at[3], halo_recv.at[3], (before, n)),
        remote(prec.at[pl.ds(24, 8)], pwin.at[pl.ds(32, 8)], halo_send.at[4], halo_recv.at[4], (after, n)),
        remote(prec.at[pl.ds(0, 8)], pwin.at[pl.ds(40, 8)], halo_send.at[5], halo_recv.at[5], (before, n)),
    ]
    to_after, to_before = halos[0::2], halos[1::2]

    def start_if(condition, copies):
        @pl.when(condition)
        def _():
            for copy in copies:
                copy.start()

    start_if(jnp.logical_not(first_band), to_before)
    start_if(last_band, to_after)

    def send_states(chunk):
        for index, _ in peers:
            start = pl.multiple_of(index * CELLS + chunk * CHUNK, CHUNK)
            remote(states.at[:, pl.ds(start, CHUNK)],
                   inbuf.at[mine, pl.ds(pl.multiple_of(chunk * CHUNK, CHUNK), CHUNK)],
                   in_send.at[chunk], in_recv.at[chunk], (w, index)).start()

    left, right = (0, LEFT), (LEFT, WIN - LEFT)
    half = (WIN - LEFT) // 2
    right_low, right_high = (LEFT, half), (LEFT + half, half)
    moves = []

    def move(slot, count, columns, to):
        sem = len(moves)
        block = win.at[rows(slot, count), pl.ds(*columns)]
        copy = remote(block, block, obs_send.at[sem], obs_recv.at[sem], (w, at(*to)[0]))
        copy.start()
        moves.append(copy)
        return copy

    def pair(dy):
        return 4 * ((y + dy) % 4) + 2 * c

    def one(dy):
        return pair(dy) + x

    up, down, across, core = (1, 0, 0), (3, 0, 0), (0, 1, 0), (0, 0, 1)
    locals_[0].wait()
    left_x = move(one(0), 1, left, across)
    send_states(0)
    left_x.wait_recv()
    left_up = move(pair(0), 2, left, up)
    left_down = move(pair(0), 2, left, down)
    last = [move(pair(0), 2, left, core)]
    halos[1].wait_recv()
    start_if(jnp.logical_not(last_band), to_after)
    send_states(1)
    halos[0].wait_recv()
    start_if(first_band, to_before)
    right_up = move(one(0), 1, right, up)
    right_down = move(one(0), 1, right, down)
    right_x0 = move(one(0), 1, right, across)
    left_up.wait_recv()
    left_up2 = move(pair(3), 1, left, up)
    last.append(move(pair(3), 2, left, core))
    left_down.wait_recv()
    left_down2 = move(pair(1) + 1, 1, left, down)
    last.append(move(pair(1), 2, left, core))
    send_states(2)
    right_up.wait_recv()
    right_up2 = move(one(3), 1, right_low, up)
    right_x3 = move(one(3), 1, right, across)
    right_down.wait_recv()
    right_down2 = move(one(1), 1, right_high, down)
    right_x1 = move(one(1), 1, right, across)
    left_up2.wait_recv()
    left_down2.wait_recv()
    last.append(move(pair(2), 2, left, core))
    send_states(3)
    right_up2.wait_recv()
    right_down2.wait_recv()
    right_x2 = move(one(2), 1, right, across)
    right_x0.wait_recv()
    last.append(move(pair(0), 2, right, core))
    right_x3.wait_recv()
    last.append(move(pair(3), 2, right, core))
    right_x1.wait_recv()
    last.append(move(pair(1), 2, right, core))
    send_states(4)
    right_x2.wait_recv()
    last.append(move(pair(2), 2, right, core))

    @pl.loop(5, CHUNKS)
    def _(chunk):
        send_states(chunk)

    for copy in locals_[1:]:
        copy.wait()
    own_pick = picked[pl.ds(n % 8, 1), :]
    own_pick = jnp.where(
        own_pick < HALO, own_pick + OBS_W, jnp.where(own_pick < HALO + OBS_W, own_pick - HALO, own_pick)
    )
    coarse = lax.broadcasted_iota(jnp.int32, (40, NPICK), 0) == (own_pick >> 7)
    fine = lax.broadcasted_iota(jnp.int32, (LANES, NPICK), 0) == (own_pick & 127)
    tapwin[...] = lax.dot_general(
        jnp.where(coarse, tap[...], 0.0), fine.astype(jnp.float32), NT,
        precision=HIGH, preferred_element_type=jnp.float32,
    )
    gram[...] = jnp.zeros_like(gram)
    facc[...] = jnp.zeros_like(facc)
    for copy in halos[2:]:
        copy.wait_recv()
    for copy in last:
        copy.wait_recv()

    @pl.loop(0, WIN // TILE)
    def _(tile):
        columns = pl.ds(pl.multiple_of(tile * TILE, TILE), TILE)

        def flat(ref, first):
            row = 2 * tile + first * (tile // (OBS_W // TILE))
            return jnp.concatenate([ref[pl.ds(row, 1), :], ref[pl.ds(row + 1, 1), :]], axis=1)

        ensemble = win[:, columns].astype(jnp.float32)
        mean = jnp.sum(ensemble, axis=0, keepdims=True) * (1.0 / MEMBERS)
        pert = ensemble - mean
        weight = flat(pwin, 6) * flat(tapwin, 0)
        scaled = (pert * jnp.sqrt(weight)).astype(jnp.bfloat16)
        gram[...] += lax.dot_general(scaled, scaled, NT, preferred_element_type=jnp.float32)
        force = pert * (weight * (flat(vwin, 6) - mean))
        facc[...] += force[:, :LANES] + force[:, LANES:]

    identity = (
        lax.broadcasted_iota(jnp.int32, (MEMBERS, MEMBERS), 0)
        == lax.broadcasted_iota(jnp.int32, (MEMBERS, MEMBERS), 1)
    ).astype(jnp.float32)

    def dot(a, b):
        return jnp.dot(a, b, precision=HIGH, preferred_element_type=jnp.float32)

    matrix = gram[...] + (MEMBERS - 1.0) * identity
    scale = jnp.sqrt(jnp.sum(jnp.sum(matrix * matrix, axis=0, keepdims=True), axis=1, keepdims=True))
    start = matrix / scale
    first = 1.5 * identity - 0.5 * start
    gram[...] = dot(start, first)
    trans[...] = first

    @pl.loop(0, ITERS - 2)
    def _(_):
        current, root = gram[...], trans[...]
        middle = 1.5 * identity - 0.5 * dot(root, current)
        gram[...] = dot(current, middle)
        trans[...] = dot(middle, root)

    root = dot(1.5 * identity - 0.5 * dot(trans[...], gram[...]), trans[...])
    inv_root = root / jnp.sqrt(scale)
    force = lax.dot_general(
        jnp.ones((8, LANES), jnp.float32), facc[...], NT, precision=HIGH, preferred_element_type=jnp.float32
    )
    inner = lax.dot_general(force, inv_root, NT, precision=HIGH, preferred_element_type=jnp.float32)
    weights = lax.dot_general(inner, inv_root, NT, precision=HIGH, preferred_element_type=jnp.float32)
    transform = (math.sqrt(MEMBERS - 1.0) * inv_root + weights[0:1]).astype(jnp.bfloat16)
    trans[...] = transform.astype(jnp.float32)
    own_states.wait()

    @pl.loop(0, CHUNKS)
    def _(chunk):
        columns = pl.ds(pl.multiple_of(chunk * CHUNK, CHUNK), CHUNK)
        arrived = inbuf.at[pl.ds(0, MEMBERS - OWN), columns]
        pltpu.make_async_copy(arrived, arrived, in_recv.at[chunk]).wait()
        mixer = trans[...].astype(jnp.bfloat16)

        @pl.loop(0, CHUNK // TILE)
        def _(tile):
            part = pl.ds(pl.multiple_of(chunk * CHUNK + tile * TILE, TILE), TILE)
            entries = inbuf[:, part].astype(jnp.float32)
            mean = jnp.sum(entries, axis=0, keepdims=True) * (1.0 / MEMBERS)
            pert = (entries - mean).astype(jnp.bfloat16)
            mixed = jnp.dot(mixer, pert, preferred_element_type=jnp.float32)
            outbuf[:, part] = (mean + mixed).astype(jnp.bfloat16)

        target = pl.ds(pl.multiple_of(n * CELLS + chunk * CHUNK, CHUNK), CHUNK)
        for index, slot in peers:
            remote(outbuf.at[rows(slot), columns], out.at[:, target],
                   out_send.at[chunk], out_recv.at[chunk], (w, index)).start()

    own_out = pltpu.make_async_copy(
        outbuf.at[mine], out.at[:, pl.ds(pl.multiple_of(n * CELLS, CELLS), CELLS)], loc_sem.at[1]
    )
    own_out.start()
    for copy in halos:
        copy.wait_send()
    for copy in moves:
        copy.wait_send()

    @pl.loop(0, CHUNKS)
    def _(chunk):
        columns = pl.ds(pl.multiple_of(chunk * CHUNK, CHUNK), CHUNK)
        most = outbuf.at[pl.ds(0, MEMBERS - OWN), columns]
        pltpu.make_async_copy(most, most, in_send.at[chunk]).wait()
        pltpu.make_async_copy(most, most, out_send.at[chunk]).wait()
        pltpu.make_async_copy(most, most, out_recv.at[chunk]).wait()

    own_out.wait()


def body(states, obs_ens, obs_value, obs_prec, obs_pick, taper):
    anywhere = pl.BlockSpec(memory_space=pl.ANY)
    dma = pltpu.SemaphoreType.DMA

    return pl.pallas_call(
        kernel,
        out_shape=jax.ShapeDtypeStruct(states.shape, jnp.bfloat16),
        in_specs=[anywhere] * 6,
        out_specs=anywhere,
        scratch_shapes=[
            pltpu.VMEM((MEMBERS, CELLS), jnp.bfloat16),
            pltpu.VMEM((MEMBERS, CELLS), jnp.bfloat16),
            pltpu.VMEM((MEMBERS, WIN), jnp.bfloat16),
            pltpu.VMEM((48, LANES), jnp.float32),
            pltpu.VMEM((48, LANES), jnp.float32),
            pltpu.VMEM((8, NPICK), jnp.int32),
            pltpu.VMEM((1, NPICK), jnp.float32),
            pltpu.VMEM((40, LANES), jnp.float32),
            pltpu.VMEM((MEMBERS, MEMBERS), jnp.float32),
            pltpu.VMEM((MEMBERS, LANES), jnp.float32),
            pltpu.VMEM((MEMBERS, MEMBERS), jnp.float32),
            dma((CHUNKS,)),
            dma((CHUNKS,)),
            dma((CHUNKS,)),
            dma((CHUNKS,)),
            dma((7,)),
            dma((6,)),
            dma((6,)),
            dma((21,)),
            dma((21,)),
        ],
        compiler_params=pltpu.CompilerParams(
            collective_id=0, has_side_effects=True, vmem_limit_bytes=48 << 20
        ),
        name="analysis",
    )(*(pltpu.with_memory_space_constraint(a, pltpu.HBM) for a in (
        states,
        obs_ens,
        obs_value.reshape(OBS_W // LANES, LANES),
        obs_prec.reshape(OBS_W // LANES, LANES),
        obs_pick,
        taper,
    )))


def solution(mesh):
    return jax.shard_map(
        body,
        mesh=mesh,
        in_specs=(
            P("narrow", "wide"),
            P("narrow", "wide"),
            P("wide"),
            P("wide"),
            P("wide", None),
            P(("wide", "narrow"), None),
        ),
        out_specs=P("narrow", "wide"),
        check_vma=False,
    )
```
